256 devices in a mesh: rows: 32 (over y, x, core), cols: 8 (over z).
Axes of the slice: x: 4, y: 4, z: 8, core: 2. Of those that a mesh axis runs over, the one named last changes fastest.
Arguments:
- a_blocks: bfloat16 [8192, 28672], P(('rows', 'cols')), may hold values from -6 to 6
- prolong: bfloat16 [8192, 4096], P(('rows', 'cols')), may hold values from -0.75 to 0.75
- columns: int32 [8192, 7], P(('rows', 'cols')), may hold values from -1 to 8191, as said below
- aggregate: int32 [8192], P(('rows', 'cols')), may hold values from 0 to 3, as said below
Outputs:
- coarse: float32 [1024, 64, 320], P('rows', 'cols')
The draws below stay inside these ranges and needn't reach their ends.
Inputs may be any that keep to these rules, and one draw needn't show every extreme that they name: `columns`: entries that are not -1 lie within 8 block rows of their own row, and some lie exactly 8 away on each side; -1 marks padding, placed at random positions of a row. Within each block of 32 rows the ids never fall, every id 0 to 3 is used, and each aggregate has 4 to 12 rows, both reached in every such block; so glob of a valid column differs from the row's by at most 2.
All inputs are finite; a program needn't handle non-finite values.
Results may differ from the reference program's by a relative error of at most 0.0029.
Values may be sent and summed in bfloat16 or wider, within the bound.
No kernel may reach another device: no remote copies, remote signals or barrier semaphores. Data moves between devices by JAX's collectives and lax.ppermute only.
A program may use at most 64 MiB of HBM per device.

```python
import jax
import jax.numpy as jnp
from jax import lax

BW = 64
NS = 64
KN = 7
AGGR = 8
HW = 8
RC = 2
SL = 5
NB_DEV = 32
LA = 4
NB = 8192


def draw_columns(key, part):
    key = jax.random.fold_in(key, 11)
    keys = jax.random.split(key, 6)
    half = HW // 2
    row_ids = jnp.arange(NB, dtype=jnp.int32)
    zero_off = jnp.zeros((NB,), jnp.int32)
    far_low = -jax.random.randint(keys[0], (NB,), half, HW, dtype=jnp.int32)
    near_low = -jax.random.randint(keys[1], (NB,), 1, half, dtype=jnp.int32)
    near_high = jax.random.randint(keys[2], (NB,), 1, half, dtype=jnp.int32)
    far_high = jax.random.randint(keys[3], (NB,), half, HW, dtype=jnp.int32)
    offsets = jnp.stack([zero_off, zero_off - HW, zero_off + HW, far_low, near_low, near_high, far_high], axis=1)
    target = row_ids[:, None] + offsets
    dropped = (jax.random.randint(keys[4], (NB, KN), 0, 8, dtype=jnp.int32) == 0) & (jnp.arange(KN, dtype=jnp.int32)[None, :] >= 3)
    outside = (target < 0) | (target >= NB) | dropped
    entries = jnp.where(outside, -1, target)
    scores = jax.random.randint(keys[5], (NB, KN), 0, 1 << 20, dtype=jnp.int32) * KN + jnp.arange(KN, dtype=jnp.int32)[None, :]
    order = jnp.argsort(scores, axis=1, stable=True)
    return jnp.take_along_axis(entries, order, axis=1).astype(jnp.int32)


def draw_aggregate(key, part):
    key = jax.random.fold_in(key, 23)
    keys = jax.random.split(key, 3)
    devs = NB // NB_DEV
    pairs = LA // 2
    spread = jax.random.randint(keys[0], (devs, pairs), -(AGGR // 2), AGGR // 2 + 1, dtype=jnp.int32)
    forced = jax.random.randint(keys[1], (devs, 1), 0, pairs, dtype=jnp.int32)
    flip = jax.random.randint(keys[2], (devs, 1), 0, 2, dtype=jnp.int32) * 2 - 1
    pair_ids = jnp.arange(pairs, dtype=jnp.int32)[None, :]
    spread = jnp.where(pair_ids == forced, flip * (AGGR // 2), spread)
    sizes = jnp.stack([AGGR + spread, AGGR - spread], axis=2).reshape(devs, LA)
    ends = jnp.cumsum(sizes, axis=1)
    positions = jnp.arange(NB_DEV, dtype=jnp.int32)
    labels = jnp.sum((ends[:, None, :] <= positions[None, :, None]).astype(jnp.int32), axis=2)
    return labels.reshape(NB).astype(jnp.int32)


def level_of(rng, extent, shards, least, high):
    def one(axis_at, blocks):
        draws = jax.random.uniform(jax.random.fold_in(jax.random.fold_in(rng, 6), axis_at), (blocks,), jnp.float32, least / len(shards), high / len(shards))
        return jnp.repeat(jnp.exp(draws), extent[axis_at] // blocks).reshape((-1,) + (1,) * (len(extent) - axis_at - 1))

    loudness = one(*shards[0])
    for cut in shards[1:]:
        loudness = loudness * one(*cut)
    return loudness


def scatter_about(stream_key, extent, deviation, most, shards=(), kind=jnp.bfloat16):
    values = jax.random.normal(stream_key, extent, jnp.float32) * deviation
    if len(shards) > 0:
        values = level_of(stream_key, extent, shards, -0.22, 0.18) * values
    return jnp.clip(values, min=-most, max=most).astype(kind)


def setup_inputs(seed: int = 0) -> dict:
    key_list = jax.random.split(jax.random.key(seed), 5)
    a_blocks = scatter_about(key_list[0], (NB, KN * BW * BW), 1.0, 6.0, ((0, 256),))
    prolong = scatter_about(key_list[1], (NB, BW * NS), BW ** -0.5, 0.75, ((0, 256),))
    columns = draw_columns(jax.random.fold_in(key_list[4], 71), 0)
    aggregate = draw_aggregate(jax.random.fold_in(key_list[4], 71), 0)
    return {"a_blocks": a_blocks, "prolong": prolong, "columns": columns, "aggregate": aggregate}


def reference(a_blocks, prolong, columns, aggregate):
    total = a_blocks.shape[0]
    blocks = total // NB_DEV
    glob = (jnp.arange(total, dtype=jnp.int32) // NB_DEV) * LA + aggregate
    p_three = prolong.reshape(total, BW, NS)

    def one_block(index):
        start = (index * NB_DEV).astype(jnp.int32)
        a_rows = lax.dynamic_slice_in_dim(a_blocks, start, NB_DEV, 0).reshape(NB_DEV, KN, BW, BW)
        col_rows = lax.dynamic_slice_in_dim(columns, start, NB_DEV, 0)
        valid = col_rows >= 0
        safe = jnp.where(valid, col_rows, 0).astype(jnp.int32)
        gathered = p_three[safe]
        prod = jnp.einsum('tkuw,tkwv->tkuv', a_rows.astype(jnp.float32), gathered.astype(jnp.float32))
        row_glob = lax.dynamic_slice_in_dim(glob, start, NB_DEV, 0)
        slot = glob[safe] - row_glob[:, None] + RC
        onehot = ((slot[:, :, None] == jnp.arange(SL, dtype=jnp.int32)[None, None, :]) & valid[:, :, None]).astype(jnp.float32)
        grouped = jnp.einsum('tks,tkuv->tsuv', onehot, prod, precision=lax.Precision.HIGHEST).astype(jnp.bfloat16)
        own_p = lax.dynamic_slice_in_dim(p_three, start, NB_DEV, 0)
        local = jnp.einsum('twu,tswv->tsuv', own_p.astype(jnp.float32), grouped.astype(jnp.float32))
        own_agg = lax.dynamic_slice_in_dim(aggregate, start, NB_DEV, 0)
        select = (own_agg[None, :] == jnp.arange(LA, dtype=jnp.int32)[:, None]).astype(jnp.float32)
        summed = jnp.einsum('at,tsuv->avsu', select, local, precision=lax.Precision.HIGHEST)
        return summed.reshape(LA, NS, SL * NS)

    result = lax.map(one_block, jnp.arange(blocks, dtype=jnp.int32))
    return result.reshape(blocks * LA, NS, SL * NS)
```

```python
import jax
import jax.numpy as jnp
from jax import lax
from jax.experimental import pallas as pl
from jax.experimental.pallas import tpu as pltpu
from jax.sharding import PartitionSpec as P

BW = 64
NS = 64
KN = 7
HW = 8
RC = 2
SL = 5
LA = 4
NB = 32
G = 32
EXT = NB + 2 * HW
BLK = BW * BW
COLS = 8


def shifted(shard, by):
    axis = ("rows", "cols")
    length = lax.axis_size(axis)
    return lax.ppermute(shard, axis, [(i, (i + by) % length) for i in range(length)])


def halo_of(prolong, aggregate, rows):
    ids = jnp.broadcast_to(aggregate[rows].astype(jnp.bfloat16)[:, None], (HW, 128))
    return jnp.concatenate([prolong[rows], ids], axis=1)


def local_kernel(start_ref, cols_ref, agg_ref, a_hbm, p_ref, lo_ref, hi_ref, out_ref,
                 a_vmem, a_nat, p_nat, w_wide, w_blk, p_sel, acc, glob, y_buf, sems):
    copies = [
        pltpu.make_async_copy(a_hbm.at[:, pl.ds(k * BLK, BLK)], a_vmem.at[:, pl.ds(k * BLK, BLK)], sems.at[k])
        for k in range(KN)
    ]
    for c in copies:
        c.start()
    start = start_ref[0]

    below = jnp.max(jnp.sum((lo_ref[:, pl.ds(BLK, 128)].astype(jnp.float32) > 2.5).astype(jnp.float32), axis=0)).astype(jnp.int32)
    above = jnp.max(jnp.sum((hi_ref[:, pl.ds(BLK, 128)].astype(jnp.float32) < 0.5).astype(jnp.float32), axis=0)).astype(jnp.int32)
    for t in range(HW):
        glob[t] = jnp.where(HW - t <= below, -1, -2)
        glob[HW + NB + t] = jnp.where(t < above, LA, LA + 1)
    for t in range(NB):
        glob[HW + t] = agg_ref[t]

    for h in range(G):
        lanes = pl.ds(h * 128, 128)
        p_nat[pl.ds(h * EXT, HW), :] = lo_ref[:, lanes].astype(jnp.float32)
        p_nat[pl.ds(h * EXT + HW, NB), :] = p_ref[:, lanes].astype(jnp.float32)
        p_nat[pl.ds(h * EXT + HW + NB, HW), :] = hi_ref[:, lanes].astype(jnp.float32)
    low = lax.broadcasted_iota(jnp.int32, (G, 128), 1) < NS
    p_sel[...] = jnp.zeros_like(p_sel)
    for j in range(EXT):
        nat = p_nat[pl.ds(j, G, stride=EXT), :]
        even = jnp.where(low, nat, 0.0)
        odd = jnp.where(low, 0.0, nat)
        w_wide[j, pl.ds(0, G, stride=2), :] = even
        w_wide[j, pl.ds(1, G, stride=2), :] = pltpu.roll(odd, NS, 1)
        w_wide[j, pl.ds(BW, G, stride=2), :] = pltpu.roll(even, NS, 1)
        w_wide[j, pl.ds(BW + 1, G, stride=2), :] = odd
        w_blk[j] = w_wide[j].astype(jnp.bfloat16)
        if HW <= j < HW + NB:
            i = j - HW
            lane = pl.multiple_of(agg_ref[i] * 128, 128)
            p_sel[pl.ds(i * G, G), pl.ds(lane, 128)] = nat.astype(jnp.bfloat16)
    w_blk[EXT] = jnp.zeros((128, 128), jnp.bfloat16)
    acc[...] = jnp.zeros_like(acc)

    for k in range(KN):
        copies[k].wait()
        for g in range(G):
            a_nat[k, pl.ds(g * NB, NB), :] = a_vmem[:, pl.ds(k * BLK + g * 128, 128)].astype(jnp.float32)
        for i in range(NB):
            block = a_nat[k, pl.ds(i, G, stride=NB), :].astype(jnp.bfloat16)
            col = cols_ref[k, i]
            valid = col >= 0
            j = jnp.where(valid, col - start + HW, EXT)
            slot = jnp.where(valid, glob[jnp.where(valid, j, 0)] - agg_ref[i] + RC, RC)
            prod = jnp.dot(block, w_blk[j], preferred_element_type=jnp.float32)
            lane = pl.multiple_of(slot * 128, 128)
            acc[pl.ds(i * G, G), pl.ds(lane, 128)] += prod

    full = lax.dot_general(acc[...].astype(jnp.bfloat16), p_sel[...], (((0,), (0,)), ((), ())),
                           preferred_element_type=jnp.float32)
    low = lax.broadcasted_iota(jnp.int32, (NS, 128), 1) < NS
    for c in range(LA):
        cc = full[:, c * 128:(c + 1) * 128]
        part = lambda s, par: cc[s * 128 + par * NS:s * 128 + (par + 1) * NS]
        for pair in range(3):
            s0, s1 = 2 * pair, min(2 * pair + 1, SL - 1)
            stay = jnp.where(low, part(s0, 0), part(s1, 1))
            move = jnp.where(low, part(s1, 0), part(s0, 1))
            both = stay + pltpu.roll(move, NS, 1)
            y_buf[:, pl.ds(c * 8, 8), pl.ds(pair * 128, 128)] = both.reshape(8, 8, 128)
    out_ref[...] = y_buf[:, :, :SL * NS].astype(jnp.bfloat16)


def local_part(start, columns_t, aggregate, a_blocks, prolong, lo, hi):
    vmem = pl.BlockSpec(memory_space=pltpu.VMEM)
    smem = pl.BlockSpec(memory_space=pltpu.SMEM)
    return pl.pallas_call(
        local_kernel,
        out_shape=jax.ShapeDtypeStruct((COLS, LA * NS // COLS, SL * NS), jnp.bfloat16),
        in_specs=[smem, smem, smem, pl.BlockSpec(memory_space=pl.ANY), vmem, vmem, vmem],
        out_specs=vmem,
        scratch_shapes=[
            pltpu.VMEM((NB, KN * BLK), jnp.bfloat16),
            pltpu.VMEM((KN, G * NB, 128), jnp.float32),
            pltpu.VMEM((G * EXT, 128), jnp.float32),
            pltpu.VMEM((EXT, 128, 128), jnp.float32),
            pltpu.VMEM((EXT + 1, 128, 128), jnp.bfloat16),
            pltpu.VMEM((NB * G, LA * 128), jnp.bfloat16),
            pltpu.VMEM((NB * G, SL * 128), jnp.float32),
            pltpu.SMEM((EXT,), jnp.int32),
            pltpu.VMEM((COLS, LA * NS // COLS, 3 * 128), jnp.float32),
            pltpu.SemaphoreType.DMA((KN,)),
        ],
        compiler_params=pltpu.CompilerParams(vmem_limit_bytes=40 * 1024 * 1024),
    )(start, columns_t, aggregate, a_blocks, prolong, lo, hi)


def shards(a_blocks, prolong, columns, aggregate):
    count = prolong.shape[0]
    device = lax.axis_index(("rows", "cols"))
    start = (device * count).astype(jnp.int32).reshape(1)
    lo = shifted(halo_of(prolong, aggregate, slice(count - HW, count)), 1)
    hi = shifted(halo_of(prolong, aggregate, slice(0, HW)), -1)
    mine = local_part(start, columns.T, aggregate, a_blocks, prolong, lo, hi)
    landed = lax.all_to_all(mine, "cols", split_axis=0, concat_axis=0, tiled=True)
    return landed.astype(jnp.float32).reshape(COLS * LA, NS // COLS, SL * NS)


def solution(mesh):
    in_specs = (
        P(("rows", "cols"), None),
        P(("rows", "cols"), None),
        P(("rows", "cols"), None),
        P(("rows", "cols")),
    )
    out_specs = P("rows", "cols", None)
    return jax.shard_map(shards, mesh=mesh, in_specs=in_specs, out_specs=out_specs, check_vma=False)
```

```python
import jax
import jax.numpy as jnp
from jax import lax
from jax.experimental import pallas as pl
from jax.experimental.pallas import tpu as pltpu
from jax.sharding import PartitionSpec as P

BW = 64
NS = 64
KN = 7
HW = 8
RC = 2
SL = 5
LA = 4
NB = 32
G = BW // 2
BLK = BW * BW
COLS = 8
NONE = NB
LOW = NB + 1
HIGH = LOW + HW
PLACES = HIGH + HW
INNER = tuple(range(HW, NB - HW))
OUTER = tuple(range(HW)) + tuple(range(NB - HW, NB))

VMEM = pl.BlockSpec(memory_space=pltpu.VMEM)
HBM = pl.BlockSpec(memory_space=pltpu.HBM)
SMALL = pltpu.CompilerParams(vmem_limit_bytes=24 * 1024 * 1024)


def shape(dims, dtype):
    return jax.ShapeDtypeStruct(dims, dtype)


def low_lanes(rows):
    return lax.broadcasted_iota(jnp.int32, (rows, 128), 1) < NS


def load_kernel(p_hbm, agg_hbm, cols_hbm, a_hbm, down_ref, up_ref, place_ref, agg_ref, p_ref, a_ref, agg_s, sems):
    p_in = pltpu.make_async_copy(p_hbm, p_ref, sems.at[0])
    ids_in = pltpu.make_async_copy(agg_hbm, agg_s, sems.at[1])
    cols_in = pltpu.make_async_copy(cols_hbm, place_ref, sems.at[2])
    agg_in = pltpu.make_async_copy(agg_hbm, agg_ref, sems.at[3])
    a_in = pltpu.make_async_copy(a_hbm, a_ref, sems.at[4])
    for c in (p_in, ids_in, cols_in, agg_in, a_in):
        c.start()
    ids_in.wait()
    last, first = jnp.int32(0), jnp.int32(0)
    for t in range(HW):
        last += (agg_s[NB - HW + t] == LA - 1).astype(jnp.int32)
        first += (agg_s[t] == 0).astype(jnp.int32)
    down_ref[:, BLK:] = jnp.full((HW, 128), first.astype(jnp.float32), jnp.float32).astype(jnp.bfloat16)
    up_ref[:, BLK:] = jnp.full((HW, 128), last.astype(jnp.float32), jnp.float32).astype(jnp.bfloat16)
    cols_in.wait()
    cols = place_ref[...]
    row = lax.broadcasted_iota(jnp.int32, cols.shape, 1)
    rel = row + jnp.bitwise_and(cols - row + HW, NB - 1) - HW
    place = jnp.where(rel < 0, rel + HW + LOW, jnp.where(rel < NB, rel, rel - NB + HIGH))
    place_ref[...] = jnp.where(cols < 0, NONE, place)
    p_in.wait()
    down_ref[:, :BLK] = p_ref[:HW, :]
    up_ref[:, :BLK] = p_ref[NB - HW:, :]
    agg_in.wait()
    a_in.wait()


def widen(nat, wide, low):
    even = jnp.where(low, nat, 0.0)
    odd = jnp.where(low, 0.0, nat)
    wide[pl.ds(0, G, stride=2), :] = even
    wide[pl.ds(1, G, stride=2), :] = pltpu.roll(odd, NS, 1)
    wide[pl.ds(BW, G, stride=2), :] = pltpu.roll(even, NS, 1)
    wide[pl.ds(BW + 1, G, stride=2), :] = odd


def products(rows, a_nat, w_ref, place_s, slot_of, acc):
    for k in range(KN):
        for at, i in enumerate(rows):
            block = a_nat[k, pl.ds(i, G, stride=NB), :].astype(jnp.bfloat16)
            place = place_s[k, i]
            lane = pl.multiple_of(slot_of(place, i) * 128, 128)
            acc[pl.ds(at * G, G), pl.ds(lane, 128)] += jnp.dot(block, w_ref[place], preferred_element_type=jnp.float32)


def onto_coarse(acc, sel_ref):
    return lax.dot_general(acc[...].astype(jnp.bfloat16), sel_ref[...], (((0,), (0,)), ((), ())),
                           preferred_element_type=jnp.float32)


def inner_kernel(place_v, agg_v, p_ref, a_ref, a_nat, w_ref, sel_outer, part_ref,
                 p_nat, wide, sel_inner, acc, place_s, agg_s, sems):
    place_in = pltpu.make_async_copy(place_v, place_s, sems.at[0])
    agg_in = pltpu.make_async_copy(agg_v, agg_s, sems.at[1])
    place_in.start()
    agg_in.start()
    acc[...] = jnp.zeros_like(acc)
    sel_inner[...] = jnp.zeros_like(sel_inner)
    sel_outer[...] = jnp.zeros_like(sel_outer)
    for h in range(G):
        p_nat[pl.ds(h * NB, NB), :] = p_ref[:, pl.ds(h * 128, 128)].astype(jnp.float32)
    place_in.wait()
    agg_in.wait()
    low = low_lanes(G)
    for j in range(NB):
        nat = p_nat[pl.ds(j, G, stride=NB), :]
        widen(nat, wide.at[j], low)
        w_ref[j] = wide[j].astype(jnp.bfloat16)
        lane = pl.multiple_of(agg_s[j] * 128, 128)
        if j in INNER:
            sel_inner[pl.ds(INNER.index(j) * G, G), pl.ds(lane, 128)] = nat.astype(jnp.bfloat16)
        else:
            sel_outer[pl.ds(OUTER.index(j) * G, G), pl.ds(lane, 128)] = nat.astype(jnp.bfloat16)
    w_ref[NONE] = jnp.zeros((128, 128), jnp.bfloat16)
    for k in range(KN):
        for g in range(G):
            a_nat[k, pl.ds(g * NB, NB), :] = a_ref[:, pl.ds(k * BLK + g * 128, 128)].astype(jnp.float32)

    def slot_of(place, i):
        return jnp.where(place < NB, agg_s[jnp.minimum(place, NB - 1)] - agg_s[i] + RC, RC)

    products(INNER, a_nat, w_ref, place_s, slot_of, acc)
    part_ref[...] = onto_coarse(acc, sel_inner)


def outer_kernel(place_v, agg_v, lo_ref, hi_ref, a_nat, w_own, sel_outer, part_ref, out_ref,
                 p_nat, wide, w_all, acc, y_buf, place_s, agg_s, glob, sems):
    place_in = pltpu.make_async_copy(place_v, place_s, sems.at[0])
    agg_in = pltpu.make_async_copy(agg_v, agg_s, sems.at[1])
    place_in.start()
    agg_in.start()
    below = jnp.max(lo_ref[:, BLK:].astype(jnp.float32)).astype(jnp.int32)
    above = jnp.max(hi_ref[:, BLK:].astype(jnp.float32)).astype(jnp.int32)
    acc[...] = jnp.zeros_like(acc)
    w_all[:LOW] = w_own[...]
    for h in range(G):
        lanes = pl.ds(h * 128, 128)
        p_nat[pl.ds(h * 2 * HW, HW), :] = lo_ref[:, lanes].astype(jnp.float32)
        p_nat[pl.ds(h * 2 * HW + HW, HW), :] = hi_ref[:, lanes].astype(jnp.float32)
    low = low_lanes(G)
    for j in range(2 * HW):
        widen(p_nat[pl.ds(j, G, stride=2 * HW), :], wide.at[j], low)
        w_all[LOW + j] = wide[j].astype(jnp.bfloat16)
    place_in.wait()
    agg_in.wait()
    for t in range(NB):
        glob[t] = agg_s[t]
    glob[NONE] = 1
    for t in range(HW):
        glob[LOW + t] = jnp.where(HW - t <= below, -1, -2)
        glob[HIGH + t] = jnp.where(t < above, LA, LA + 1)

    def slot_of(place, i):
        return glob[place] - agg_s[i] + RC

    products(OUTER, a_nat, w_all, place_s, slot_of, acc)
    full = part_ref[...] + onto_coarse(acc, sel_outer)
    low = low_lanes(NS)
    for c in range(LA):
        cc = full[:, c * 128:(c + 1) * 128]
        part = lambda s, par: cc[s * 128 + par * NS:s * 128 + (par + 1) * NS]
        for pair in range(3):
            s0, s1 = 2 * pair, min(2 * pair + 1, SL - 1)
            stay = jnp.where(low, part(s0, 0), part(s1, 1))
            move = jnp.where(low, part(s1, 0), part(s0, 1))
            both = stay + pltpu.roll(move, NS, 1)
            y_buf[:, pl.ds(c * 8, 8), pl.ds(pair * 128, 128)] = both.reshape(8, 8, 128)
    out_ref[...] = y_buf[:, :, :SL * NS].astype(jnp.bfloat16)


def load(prolong, aggregate, columns_t, a_blocks):
    halo = shape((HW, BLK + 128), jnp.bfloat16)
    return pl.pallas_call(
        load_kernel,
        out_shape=(halo, halo, shape((KN, NB), jnp.int32), shape((NB,), jnp.int32), shape((NB, BLK), jnp.bfloat16),
                   shape((NB, KN * BLK), jnp.bfloat16)),
        in_specs=[HBM] * 4,
        out_specs=[VMEM] * 6,
        scratch_shapes=[pltpu.SMEM((NB,), jnp.int32), pltpu.SemaphoreType.DMA((5,))],
        compiler_params=SMALL,
    )(*(pltpu.with_memory_space_constraint(x, pltpu.HBM) for x in (prolong, aggregate, columns_t, a_blocks)))


def inner(place, agg, p_v, a_v):
    n = len(INNER) * G
    return pl.pallas_call(
        inner_kernel,
        out_shape=(shape((KN, G * NB, 128), jnp.float32), shape((LOW, 128, 128), jnp.bfloat16),
                   shape((len(OUTER) * G, LA * 128), jnp.bfloat16), shape((SL * 128, LA * 128), jnp.float32)),
        in_specs=[VMEM] * 4,
        out_specs=[VMEM] * 4,
        scratch_shapes=[
            pltpu.VMEM((G * NB, 128), jnp.float32),
            pltpu.VMEM((NB, 128, 128), jnp.float32),
            pltpu.VMEM((n, LA * 128), jnp.bfloat16),
            pltpu.VMEM((n, SL * 128), jnp.float32),
            pltpu.SMEM((KN, NB), jnp.int32),
            pltpu.SMEM((NB,), jnp.int32),
            pltpu.SemaphoreType.DMA((2,)),
        ],
        compiler_params=SMALL,
    )(place, agg, p_v, a_v)


def outer(place, agg, lo, hi, a_nat, w_own, sel, part):
    return pl.pallas_call(
        outer_kernel,
        out_shape=shape((COLS, LA * NS // COLS, SL * NS), jnp.bfloat16),
        in_specs=[VMEM] * 8,
        out_specs=VMEM,
        scratch_shapes=[
            pltpu.VMEM((G * 2 * HW, 128), jnp.float32),
            pltpu.VMEM((2 * HW, 128, 128), jnp.float32),
            pltpu.VMEM((PLACES, 128, 128), jnp.bfloat16),
            pltpu.VMEM((len(OUTER) * G, SL * 128), jnp.float32),
            pltpu.VMEM((COLS, LA * NS // COLS, 3 * 128), jnp.float32),
            pltpu.SMEM((KN, NB), jnp.int32),
            pltpu.SMEM((NB,), jnp.int32),
            pltpu.SMEM((PLACES,), jnp.int32),
            pltpu.SemaphoreType.DMA((2,)),
        ],
        compiler_params=SMALL,
    )(place, agg, lo, hi, a_nat, w_own, sel, part)


def shifted(shard, by):
    axis = ("rows", "cols")
    length = lax.axis_size(axis)
    return lax.ppermute(shard, axis, [(i, (i + by) % length) for i in range(length)])


def shards(a_blocks, prolong, columns, aggregate):
    down, up, place, agg, p_v, a_v = load(prolong, aggregate, columns.T, a_blocks)
    lo = shifted(up, 1)
    hi = shifted(down, -1)
    mid = inner(place, agg, p_v, a_v)
    mine = outer(place, agg, lo, hi, *mid)
    landed = lax.all_to_all(mine, "cols", split_axis=0, concat_axis=0, tiled=True)
    return landed.astype(jnp.float32).reshape(COLS * LA, NS // COLS, SL * NS)


def solution(mesh):
    in_specs = (
        P(("rows", "cols"), None),
        P(("rows", "cols"), None),
        P(("rows", "cols"), None),
        P(("rows", "cols")),
    )
    out_specs = P("rows", "cols", None)
    return jax.shard_map(shards, mesh=mesh, in_specs=in_specs, out_specs=out_specs, check_vma=False)
```

```python
import jax
import jax.numpy as jnp
from jax import lax
from jax.experimental import pallas as pl
from jax.experimental.pallas import tpu as pltpu
from jax.sharding import PartitionSpec as P

BW = 64
NS = 64
KN = 7
HW = 8
RC = 2
SL = 5
LA = 4
NB = 32
G = BW // 2
BLK = BW * BW
COLS = 8
NONE = NB
LOW = NB + 1
HIGH = LOW + HW
PLACES = HIGH + HW
STEP = NB + 8
HALO_STEP = 2 * HW + 8
IDS = ((0, 2), (0, 3), (1, 3), (2, 2))
INNER = tuple(range(HW, NB - HW))
OUTER = tuple(range(HW)) + tuple(range(NB - HW, NB))

VMEM = pl.BlockSpec(memory_space=pltpu.VMEM)
HBM = pl.BlockSpec(memory_space=pltpu.HBM)
SMALL = pltpu.CompilerParams(vmem_limit_bytes=24 * 1024 * 1024)


def shape(dims, dtype):
    return jax.ShapeDtypeStruct(dims, dtype)


def low_lanes(rows):
    return lax.broadcasted_iota(jnp.int32, (rows, 128), 1) < NS


def load_kernel(p_hbm, agg_hbm, cols_hbm, a_hbm, down_ref, up_ref, place_ref, agg_ref, p_ref, a_ref, agg_s, sems):
    p_in = pltpu.make_async_copy(p_hbm, p_ref, sems.at[0])
    ids_in = pltpu.make_async_copy(agg_hbm, agg_s, sems.at[1])
    cols_in = pltpu.make_async_copy(cols_hbm, place_ref, sems.at[2])
    agg_in = pltpu.make_async_copy(agg_hbm, agg_ref, sems.at[3])
    a_in = pltpu.make_async_copy(a_hbm, a_ref, sems.at[4])
    for c in (p_in, ids_in, cols_in, agg_in, a_in):
        c.start()
    ids_in.wait()
    last, first = jnp.int32(0), jnp.int32(0)
    for t in range(HW):
        last += (agg_s[NB - HW + t] == LA - 1).astype(jnp.int32)
        first += (agg_s[t] == 0).astype(jnp.int32)
    down_ref[:, BLK:] = jnp.full((HW, 128), first.astype(jnp.float32), jnp.float32).astype(jnp.bfloat16)
    up_ref[:, BLK:] = jnp.full((HW, 128), last.astype(jnp.float32), jnp.float32).astype(jnp.bfloat16)
    cols_in.wait()
    cols = place_ref[...]
    row = lax.broadcasted_iota(jnp.int32, cols.shape, 1)
    rel = row + jnp.bitwise_and(cols - row + HW, NB - 1) - HW
    place = jnp.where(rel < 0, rel + HW + LOW, jnp.where(rel < NB, rel, rel - NB + HIGH))
    place_ref[...] = jnp.where(cols < 0, NONE, place)
    p_in.wait()
    down_ref[:, :BLK] = p_ref[:HW, :]
    up_ref[:, :BLK] = p_ref[NB - HW:, :]
    agg_in.wait()
    a_in.wait()


def widen(nat, wide, low):
    even = jnp.where(low, nat, 0.0)
    odd = jnp.where(low, 0.0, nat)
    wide[pl.ds(0, G, stride=2), :] = even
    wide[pl.ds(1, G, stride=2), :] = pltpu.roll(odd, NS, 1)
    wide[pl.ds(BW, G, stride=2), :] = pltpu.roll(even, NS, 1)
    wide[pl.ds(BW + 1, G, stride=2), :] = odd


def products(rows, a_nat, w_ref, place_s, slot_of, accs):
    for k in range(KN):
        for i, acc in zip(rows, accs):
            block = a_nat[k, pl.ds(i, G, stride=STEP), :].astype(jnp.bfloat16)
            place = place_s[k, i]
            slot = slot_of(place, i)
            acc[slot] += jnp.dot(block, w_ref[place], preferred_element_type=jnp.float32)


def onto_coarse(groups, accs, sels):
    sums = {}
    low = low_lanes(NS)
    for at, group in enumerate(groups):
        first, count = IDS[group]
        mine = accs[at * 8:at * 8 + 8]
        rows = [jnp.concatenate([acc[s] for s in range(SL)], axis=1).astype(jnp.bfloat16) for acc in mine]
        full = lax.dot_general(jnp.concatenate(rows, axis=0), sels[at][...], (((0,), (0,)), ((), ())),
                               preferred_element_type=jnp.float32)
        for c in range(count):
            cc = full[:, c * 128:(c + 1) * 128]
            part = lambda s, par: cc[s * 128 + par * NS:s * 128 + (par + 1) * NS]
            for pair in range(3):
                s0, s1 = 2 * pair, min(2 * pair + 1, SL - 1)
                stay = jnp.where(low, part(s0, 0), part(s1, 1))
                move = jnp.where(low, part(s1, 0), part(s0, 1))
                both = stay + pltpu.roll(move, NS, 1)
                key = (first + c, pair)
                sums[key] = sums[key] + both if key in sums else both
    return sums


def inner_kernel(place_v, agg_v, p_ref, a_ref, a_nat, w_ref, sel_a, sel_d, part_ref, *scratch):
    p_nat, wide, sel_b, sel_c, place_s, agg_s, glob, sems = scratch[:8]
    accs = scratch[8:]
    place_in = pltpu.make_async_copy(place_v, place_s, sems.at[0])
    agg_in = pltpu.make_async_copy(agg_v, agg_s, sems.at[1])
    place_in.start()
    agg_in.start()
    for acc in accs:
        acc[...] = jnp.zeros_like(acc)
    sels = (sel_a, sel_b, sel_c, sel_d)
    for sel in sels:
        sel[...] = jnp.zeros_like(sel)
    for h in range(G):
        p_nat[pl.ds(h * STEP, NB), :] = p_ref[:, pl.ds(h * 128, 128)].astype(jnp.float32)
    place_in.wait()
    agg_in.wait()
    for t in range(NB):
        glob[t] = agg_s[t]
    glob[NONE] = 1
    low = low_lanes(G)
    for j in range(NB):
        nat = p_nat[pl.ds(j, G, stride=STEP), :]
        widen(nat, wide.at[j], low)
        w_ref[j] = wide[j].astype(jnp.bfloat16)
        lane = pl.multiple_of((agg_s[j] - IDS[j // 8][0]) * 128, 128)
        sels[j // 8][pl.ds(j % 8 * G, G), pl.ds(lane, 128)] = nat.astype(jnp.bfloat16)
    w_ref[NONE] = jnp.zeros((128, 128), jnp.bfloat16)
    for k in range(KN):
        for g in range(G):
            a_nat[k, pl.ds(g * STEP, NB), :] = a_ref[:, pl.ds(k * BLK + g * 128, 128)].astype(jnp.float32)

    products(INNER, a_nat, w_ref, place_s, lambda place, i: glob[place] - agg_s[i] + RC, accs)
    for (c, pair), value in onto_coarse((1, 2), accs, (sel_b, sel_c)).items():
        part_ref[:, pl.ds(c * 8, 8), pl.ds(pair * 128, 128)] = value.reshape(8, 8, 128)


def outer_kernel(place_v, agg_v, lo_ref, hi_ref, a_nat, w_own, sel_a, sel_d, part_ref, out_ref, *scratch):
    p_nat, wide, w_all, place_s, agg_s, glob, sems = scratch[:7]
    accs = scratch[7:]
    place_in = pltpu.make_async_copy(place_v, place_s, sems.at[0])
    agg_in = pltpu.make_async_copy(agg_v, agg_s, sems.at[1])
    place_in.start()
    agg_in.start()
    below = jnp.max(lo_ref[:, BLK:].astype(jnp.float32)).astype(jnp.int32)
    above = jnp.max(hi_ref[:, BLK:].astype(jnp.float32)).astype(jnp.int32)
    for acc in accs:
        acc[...] = jnp.zeros_like(acc)
    for h in range(G):
        lanes = pl.ds(h * 128, 128)
        p_nat[pl.ds(h * HALO_STEP, HW), :] = lo_ref[:, lanes].astype(jnp.float32)
        p_nat[pl.ds(h * HALO_STEP + HW, HW), :] = hi_ref[:, lanes].astype(jnp.float32)
    w_all[:LOW] = w_own[...]
    low = low_lanes(G)
    for j in range(2 * HW):
        widen(p_nat[pl.ds(j, G, stride=HALO_STEP), :], wide.at[j], low)
        w_all[LOW + j] = wide[j].astype(jnp.bfloat16)
    place_in.wait()
    agg_in.wait()
    for t in range(NB):
        glob[t] = agg_s[t]
    glob[NONE] = 1
    for t in range(HW):
        glob[LOW + t] = jnp.where(HW - t <= below, -1, -2)
        glob[HIGH + t] = jnp.where(t < above, LA, LA + 1)
    products(OUTER, a_nat, w_all, place_s, lambda place, i: glob[place] - agg_s[i] + RC, accs)
    sums = onto_coarse((0, 3), accs, (sel_a, sel_d))
    for c in range(0, LA, 2):
        for pair in range(3):
            lanes = min(128, SL * NS - pair * 128)
            both = jnp.concatenate([sums[c, pair].reshape(8, 8, 128), sums[c + 1, pair].reshape(8, 8, 128)], axis=1)
            both = both + part_ref[:, pl.ds(c * 8, 16), pl.ds(pair * 128, 128)]
            out_ref[:, pl.ds(c * 8, 16), pl.ds(pair * 128, lanes)] = both[:, :, :lanes].astype(jnp.bfloat16)


def load(prolong, aggregate, columns_t, a_blocks):
    halo = shape((HW, BLK + 128), jnp.bfloat16)
    return pl.pallas_call(
        load_kernel,
        out_shape=(halo, halo, shape((KN, NB), jnp.int32), shape((NB,), jnp.int32), shape((NB, BLK), jnp.bfloat16),
                   shape((NB, KN * BLK), jnp.bfloat16)),
        in_specs=[HBM] * 4,
        out_specs=[VMEM] * 6,
        scratch_shapes=[pltpu.SMEM((NB,), jnp.int32), pltpu.SemaphoreType.DMA((5,))],
        compiler_params=SMALL,
    )(*(pltpu.with_memory_space_constraint(x, pltpu.HBM) for x in (prolong, aggregate, columns_t, a_blocks)))


def sel_shape(group):
    return 8 * G, IDS[group][1] * 128


def inner(place, agg, p_v, a_v):
    return pl.pallas_call(
        inner_kernel,
        out_shape=(shape((KN, G * STEP, 128), jnp.float32), shape((LOW, 128, 128), jnp.bfloat16),
                   shape(sel_shape(0), jnp.bfloat16), shape(sel_shape(3), jnp.bfloat16),
                   shape((COLS, LA * NS // COLS, 3 * 128), jnp.float32)),
        in_specs=[VMEM] * 4,
        out_specs=[VMEM] * 5,
        scratch_shapes=[
            pltpu.VMEM((G * STEP, 128), jnp.float32),
            pltpu.VMEM((NB, 128, 128), jnp.float32),
            pltpu.VMEM(sel_shape(1), jnp.bfloat16),
            pltpu.VMEM(sel_shape(2), jnp.bfloat16),
            pltpu.SMEM((KN, NB), jnp.int32),
            pltpu.SMEM((NB,), jnp.int32),
            pltpu.SMEM((PLACES,), jnp.int32),
            pltpu.SemaphoreType.DMA((2,)),
        ] + [pltpu.VMEM((SL, G, 128), jnp.float32)] * len(INNER),
        compiler_params=SMALL,
    )(place, agg, p_v, a_v)


def outer(place, agg, lo, hi, *mid):
    return pl.pallas_call(
        outer_kernel,
        out_shape=shape((COLS, LA * NS // COLS, SL * NS), jnp.bfloat16),
        in_specs=[VMEM] * 9,
        out_specs=VMEM,
        scratch_shapes=[
            pltpu.VMEM((G * HALO_STEP, 128), jnp.float32),
            pltpu.VMEM((2 * HW, 128, 128), jnp.float32),
            pltpu.VMEM((PLACES, 128, 128), jnp.bfloat16),
            pltpu.SMEM((KN, NB), jnp.int32),
            pltpu.SMEM((NB,), jnp.int32),
            pltpu.SMEM((PLACES,), jnp.int32),
            pltpu.SemaphoreType.DMA((2,)),
        ] + [pltpu.VMEM((SL, G, 128), jnp.float32)] * len(OUTER),
        compiler_params=SMALL,
    )(place, agg, lo, hi, *mid)


def shifted(shard, by):
    axis = ("rows", "cols")
    length = lax.axis_size(axis)
    return lax.ppermute(shard, axis, [(i, (i + by) % length) for i in range(length)])


def shards(a_blocks, prolong, columns, aggregate):
    down, up, place, agg, p_v, a_v = load(prolong, aggregate, columns.T, a_blocks)
    lo = shifted(up, 1)
    hi = shifted(down, -1)
    mid = inner(place, agg, p_v, a_v)
    mine = outer(place, agg, lo, hi, *mid)
    landed = lax.all_to_all(mine, "cols", split_axis=0, concat_axis=0, tiled=True)
    return landed.astype(jnp.float32).reshape(COLS * LA, NS // COLS, SL * NS)


def solution(mesh):
    in_specs = (
        P(("rows", "cols"), None),
        P(("rows", "cols"), None),
        P(("rows", "cols"), None),
        P(("rows", "cols")),
    )
    out_specs = P("rows", "cols", None)
    return jax.shard_map(shards, mesh=mesh, in_specs=in_specs, out_specs=out_specs, check_vma=False)
```

```python
import jax
import jax.numpy as jnp
from jax import lax
from jax.experimental import pallas as pl
from jax.experimental.pallas import tpu as pltpu
from jax.sharding import PartitionSpec as P

BW = 64
NS = 64
KN = 7
HW = 8
RC = 2
SL = 5
LA = 4
NB = 32
G = BW // 2
BLK = BW * BW
COLS = 8
NONE = NB
LOW = NB + 1
HIGH = LOW + HW
PLACES = HIGH + HW
STEP = NB + 8
HALO_STEP = 2 * HW + 8
IDS = ((0, 2), (0, 3), (1, 3), (2, 2))
INNER = tuple(range(HW, NB - HW))
OUTER = tuple(range(HW)) + tuple(range(NB - HW, NB))

VMEM = pl.BlockSpec(memory_space=pltpu.VMEM)
HBM = pl.BlockSpec(memory_space=pltpu.HBM)
SMALL = pltpu.CompilerParams(vmem_limit_bytes=24 * 1024 * 1024)


def shape(dims, dtype):
    return jax.ShapeDtypeStruct(dims, dtype)


def low_lanes(rows):
    return lax.broadcasted_iota(jnp.int32, (rows, 128), 1) < NS


def load_kernel(p_hbm, agg_hbm, cols_hbm, a_hbm, down_ref, up_ref, place_ref, agg_ref, p_ref, a_ref, agg_s, sems):
    p_in = pltpu.make_async_copy(p_hbm, p_ref, sems.at[0])
    ids_in = pltpu.make_async_copy(agg_hbm, agg_s, sems.at[1])
    cols_in = pltpu.make_async_copy(cols_hbm, place_ref, sems.at[2])
    agg_in = pltpu.make_async_copy(agg_hbm, agg_ref, sems.at[3])
    a_in = pltpu.make_async_copy(a_hbm, a_ref, sems.at[4])
    for c in (p_in, ids_in, cols_in, agg_in, a_in):
        c.start()
    ids_in.wait()
    last, first = jnp.int32(0), jnp.int32(0)
    for t in range(HW):
        last += (agg_s[NB - HW + t] == LA - 1).astype(jnp.int32)
        first += (agg_s[t] == 0).astype(jnp.int32)
    down_ref[:, BLK:] = jnp.full((HW, 128), first.astype(jnp.float32), jnp.float32).astype(jnp.bfloat16)
    up_ref[:, BLK:] = jnp.full((HW, 128), last.astype(jnp.float32), jnp.float32).astype(jnp.bfloat16)
    cols_in.wait()
    cols = place_ref[...]
    row = lax.broadcasted_iota(jnp.int32, cols.shape, 1)
    rel = row + jnp.bitwise_and(cols - row + HW, NB - 1) - HW
    place = jnp.where(rel < 0, rel + HW + LOW, jnp.where(rel < NB, rel, rel - NB + HIGH))
    place_ref[...] = jnp.where(cols < 0, NONE, place)
    p_in.wait()
    down_ref[:, :BLK] = p_ref[:HW, :]
    up_ref[:, :BLK] = p_ref[NB - HW:, :]
    agg_in.wait()
    a_in.wait()


def widen(nat, wide, low):
    even = jnp.where(low, nat, 0.0)
    odd = jnp.where(low, 0.0, nat)
    wide[pl.ds(0, G, stride=2), :] = even
    wide[pl.ds(1, G, stride=2), :] = pltpu.roll(odd, NS, 1)
    wide[pl.ds(BW, G, stride=2), :] = pltpu.roll(even, NS, 1)
    wide[pl.ds(BW + 1, G, stride=2), :] = odd


def products(rows, a_nat, w_ref, place_s, slot_of, accs):
    for k in range(KN):
        for i, acc in zip(rows, accs):
            block = a_nat[k, pl.ds(i, G, stride=STEP), :].astype(jnp.bfloat16)
            place = place_s[k, i]
            slot = slot_of(place, i)
            acc[slot] += jnp.dot(block, w_ref[place], preferred_element_type=jnp.float32)


def onto_coarse(groups, accs, sels):
    sums = {}
    low = low_lanes(NS)
    for at, group in enumerate(groups):
        first, count = IDS[group]
        mine = accs[at * 8:at * 8 + 8]
        rows = [jnp.concatenate([acc[s] for s in range(SL)], axis=1).astype(jnp.bfloat16) for acc in mine]
        full = lax.dot_general(jnp.concatenate(rows, axis=0), sels[at][...], (((0,), (0,)), ((), ())),
                               preferred_element_type=jnp.float32)
        for c in range(count):
            cc = full[:, c * 128:(c + 1) * 128]
            part = lambda s, par: cc[s * 128 + par * NS:s * 128 + (par + 1) * NS]
            for pair in range(3):
                s0, s1 = 2 * pair, min(2 * pair + 1, SL - 1)
                stay = jnp.where(low, part(s0, 0), part(s1, 1))
                move = jnp.where(low, part(s1, 0), part(s0, 1))
                both = stay + pltpu.roll(move, NS, 1)
                key = (first + c, pair)
                sums[key] = sums[key] + both if key in sums else both
    return sums


def inner_kernel(place_v, agg_v, p_ref, a_ref, a_nat, w_ref, sel_a, sel_d, part_ref, *scratch):
    p_nat, wide, sel_b, sel_c, place_s, agg_s, glob, sems = scratch[:8]
    accs = scratch[8:]
    place_in = pltpu.make_async_copy(place_v, place_s, sems.at[0])
    agg_in = pltpu.make_async_copy(agg_v, agg_s, sems.at[1])
    place_in.start()
    agg_in.start()
    for acc in accs:
        acc[...] = jnp.zeros_like(acc)
    sels = (sel_a, sel_b, sel_c, sel_d)
    for sel in sels:
        sel[...] = jnp.zeros_like(sel)
    for h in range(G):
        p_nat[pl.ds(h * STEP, NB), :] = p_ref[:, pl.ds(h * 128, 128)].astype(jnp.float32)
    place_in.wait()
    agg_in.wait()
    for t in range(NB):
        glob[t] = agg_s[t]
    glob[NONE] = 1
    low = low_lanes(G)
    for j in range(NB):
        nat = p_nat[pl.ds(j, G, stride=STEP), :]
        widen(nat, wide.at[j], low)
        w_ref[j] = wide[j].astype(jnp.bfloat16)
        lane = pl.multiple_of((agg_s[j] - IDS[j // 8][0]) * 128, 128)
        sels[j // 8][pl.ds(j % 8 * G, G), pl.ds(lane, 128)] = nat.astype(jnp.bfloat16)
    w_ref[NONE] = jnp.zeros((128, 128), jnp.bfloat16)
    for k in range(KN):
        for g in range(G):
            a_nat[k, pl.ds(g * STEP, NB), :] = a_ref[:, pl.ds(k * BLK + g * 128, 128)].astype(jnp.float32)

    products(INNER, a_nat, w_ref, place_s, lambda place, i: glob[place] - agg_s[i] + RC, accs)
    for (c, pair), value in onto_coarse((1, 2), accs, (sel_b, sel_c)).items():
        part_ref[:, pl.ds(c * 8, 8), pl.ds(pair * 128, 128)] = value.reshape(8, 8, 128)


def outer_kernel(place_v, agg_v, lo_ref, hi_ref, a_nat, w_own, sel_a, sel_d, part_ref, out_ref, *scratch):
    p_nat, wide, w_all, place_s, agg_s, glob, sems = scratch[:7]
    accs = scratch[7:]
    place_in = pltpu.make_async_copy(place_v, place_s, sems.at[0])
    agg_in = pltpu.make_async_copy(agg_v, agg_s, sems.at[1])
    place_in.start()
    agg_in.start()
    below = jnp.max(lo_ref[:, BLK:].astype(jnp.float32)).astype(jnp.int32)
    above = jnp.max(hi_ref[:, BLK:].astype(jnp.float32)).astype(jnp.int32)
    for acc in accs:
        acc[...] = jnp.zeros_like(acc)
    for h in range(G):
        lanes = pl.ds(h * 128, 128)
        p_nat[pl.ds(h * HALO_STEP, HW), :] = lo_ref[:, lanes].astype(jnp.float32)
        p_nat[pl.ds(h * HALO_STEP + HW, HW), :] = hi_ref[:, lanes].astype(jnp.float32)
    w_all[:LOW] = w_own[...]
    low = low_lanes(G)
    for j in range(2 * HW):
        widen(p_nat[pl.ds(j, G, stride=HALO_STEP), :], wide.at[j], low)
        w_all[LOW + j] = wide[j].astype(jnp.bfloat16)
    place_in.wait()
    agg_in.wait()
    for t in range(NB):
        glob[t] = agg_s[t]
    glob[NONE] = 1
    for t in range(HW):
        glob[LOW + t] = jnp.where(HW - t <= below, -1, -2)
        glob[HIGH + t] = jnp.where(t < above, LA, LA + 1)
    products(OUTER, a_nat, w_all, place_s, lambda place, i: glob[place] - agg_s[i] + RC, accs)
    sums = onto_coarse((0, 3), accs, (sel_a, sel_d))
    for c in range(0, LA, 2):
        for pair in range(3):
            lanes = min(128, SL * NS - pair * 128)
            both = jnp.concatenate([sums[c, pair].reshape(8, 8, 128), sums[c + 1, pair].reshape(8, 8, 128)], axis=1)
            both = both + part_ref[:, pl.ds(c * 8, 16), pl.ds(pair * 128, 128)]
            out_ref[:, pl.ds(c * 8, 16), pl.ds(pair * 128, lanes)] = both[:, :, :lanes].astype(jnp.bfloat16)


def load(prolong, aggregate, columns_t, a_blocks):
    halo = shape((HW, BLK + 128), jnp.bfloat16)
    return pl.pallas_call(
        load_kernel,
        out_shape=(halo, halo, shape((KN, NB), jnp.int32), shape((NB,), jnp.int32), shape((NB, BLK), jnp.bfloat16),
                   shape((NB, KN * BLK), jnp.bfloat16)),
        in_specs=[HBM] * 4,
        out_specs=[VMEM] * 6,
        scratch_shapes=[pltpu.SMEM((NB,), jnp.int32), pltpu.SemaphoreType.DMA((5,))],
        compiler_params=SMALL,
    )(*(pltpu.with_memory_space_constraint(x, pltpu.HBM) for x in (prolong, aggregate, columns_t, a_blocks)))


def sel_shape(group):
    return 8 * G, IDS[group][1] * 128


def inner(place, agg, p_v, a_v):
    return pl.pallas_call(
        inner_kernel,
        out_shape=(shape((KN, G * STEP, 128), jnp.float32), shape((LOW, 128, 128), jnp.bfloat16),
                   shape(sel_shape(0), jnp.bfloat16), shape(sel_shape(3), jnp.bfloat16),
                   shape((COLS, LA * NS // COLS, 3 * 128), jnp.float32)),
        in_specs=[VMEM] * 4,
        out_specs=[VMEM] * 5,
        scratch_shapes=[
            pltpu.VMEM((G * STEP, 128), jnp.float32),
            pltpu.VMEM((NB, 128, 128), jnp.float32),
            pltpu.VMEM(sel_shape(1), jnp.bfloat16),
            pltpu.VMEM(sel_shape(2), jnp.bfloat16),
            pltpu.SMEM((KN, NB), jnp.int32),
            pltpu.SMEM((NB,), jnp.int32),
            pltpu.SMEM((PLACES,), jnp.int32),
            pltpu.SemaphoreType.DMA((2,)),
        ] + [pltpu.VMEM((SL, G, 128), jnp.float32)] * len(INNER),
        compiler_params=SMALL,
    )(place, agg, p_v, a_v)


def outer(place, agg, lo, hi, *mid):
    return pl.pallas_call(
        outer_kernel,
        out_shape=shape((COLS, LA * NS // COLS, SL * NS), jnp.bfloat16),
        in_specs=[VMEM] * 9,
        out_specs=VMEM,
        scratch_shapes=[
            pltpu.VMEM((G * HALO_STEP, 128), jnp.float32),
            pltpu.VMEM((2 * HW, 128, 128), jnp.float32),
            pltpu.VMEM((PLACES, 128, 128), jnp.bfloat16),
            pltpu.SMEM((KN, NB), jnp.int32),
            pltpu.SMEM((NB,), jnp.int32),
            pltpu.SMEM((PLACES,), jnp.int32),
            pltpu.SemaphoreType.DMA((2,)),
        ] + [pltpu.VMEM((SL, G, 128), jnp.float32)] * len(OUTER),
        compiler_params=SMALL,
    )(place, agg, lo, hi, *mid)


def shifted(shard, by):
    axis = ("rows", "cols")
    length = lax.axis_size(axis)
    return lax.ppermute(shard, axis, [(i, (i + by) % length) for i in range(length)])


def shards(a_blocks, prolong, columns, aggregate):
    down, up, place, agg, p_v, a_v = load(prolong, aggregate, columns.T, a_blocks)
    hi = shifted(down, -1)
    lo = shifted(up, 1)
    mid = inner(place, agg, p_v, a_v)
    mine = outer(place, agg, lo, hi, *mid)
    landed = lax.all_to_all(mine, "cols", split_axis=0, concat_axis=0, tiled=True)
    return landed.astype(jnp.float32).reshape(COLS * LA, NS // COLS, SL * NS)


def solution(mesh):
    in_specs = (
        P(("rows", "cols"), None),
        P(("rows", "cols"), None),
        P(("rows", "cols"), None),
        P(("rows", "cols")),
    )
    out_specs = P("rows", "cols", None)
    return jax.shard_map(shards, mesh=mesh, in_specs=in_specs, out_specs=out_specs, check_vma=False)
```

```python
import jax
import jax.numpy as jnp
from jax import lax
from jax.experimental import pallas as pl
from jax.experimental.pallas import tpu as pltpu
from jax.sharding import PartitionSpec as P

BW = 64
NS = 64
KN = 7
HW = 8
RC = 2
SL = 5
LA = 4
NB = 32
G = BW // 2
BLK = BW * BW
COLS = 8
NONE = NB
LOW = NB + 1
HIGH = LOW + HW
PLACES = HIGH + HW
STEP = NB + 8
HALO_STEP = 2 * HW + 8
IDS = ((0, 2), (0, 3), (1, 3), (2, 2))
INNER = tuple(range(HW, NB - HW))
OUTER = tuple(range(HW)) + tuple(range(NB - HW, NB))

VMEM = pl.BlockSpec(memory_space=pltpu.VMEM)
HBM = pl.BlockSpec(memory_space=pltpu.HBM)
SMALL = pltpu.CompilerParams(vmem_limit_bytes=24 * 1024 * 1024)


def shape(dims, dtype):
    return jax.ShapeDtypeStruct(dims, dtype)


def low_lanes(rows):
    return lax.broadcasted_iota(jnp.int32, (rows, 128), 1) < NS


def load_kernel(p_hbm, agg_hbm, cols_hbm, a_hbm, down_ref, up_ref, place_ref, agg_ref, p_ref, a_ref, agg_s, sems):
    p_in = pltpu.make_async_copy(p_hbm, p_ref, sems.at[0])
    ids_in = pltpu.make_async_copy(agg_hbm, agg_s, sems.at[1])
    cols_in = pltpu.make_async_copy(cols_hbm, place_ref, sems.at[2])
    agg_in = pltpu.make_async_copy(agg_hbm, agg_ref, sems.at[3])
    a_in = pltpu.make_async_copy(a_hbm, a_ref, sems.at[4])
    for c in (p_in, ids_in, cols_in, agg_in, a_in):
        c.start()
    ids_in.wait()
    last, first = jnp.int32(0), jnp.int32(0)
    for t in range(HW):
        last += (agg_s[NB - HW + t] == LA - 1).astype(jnp.int32)
        first += (agg_s[t] == 0).astype(jnp.int32)
    down_ref[:, BLK:] = jnp.full((HW, 128), first.astype(jnp.float32), jnp.float32).astype(jnp.bfloat16)
    up_ref[:, BLK:] = jnp.full((HW, 128), last.astype(jnp.float32), jnp.float32).astype(jnp.bfloat16)
    cols_in.wait()
    cols = place_ref[...]
    row = lax.broadcasted_iota(jnp.int32, cols.shape, 1)
    rel = row + jnp.bitwise_and(cols - row + HW, NB - 1) - HW
    place = jnp.where(rel < 0, rel + HW + LOW, jnp.where(rel < NB, rel, rel - NB + HIGH))
    place_ref[...] = jnp.where(cols < 0, NONE, place)
    p_in.wait()
    down_ref[:, :BLK] = p_ref[:HW, :]
    up_ref[:, :BLK] = p_ref[NB - HW:, :]
    agg_in.wait()
    a_in.wait()


def widen(nat, wide, low):
    even = jnp.where(low, nat, 0.0)
    odd = jnp.where(low, 0.0, nat)
    wide[pl.ds(0, G, stride=2), :] = even
    wide[pl.ds(1, G, stride=2), :] = pltpu.roll(odd, NS, 1)
    wide[pl.ds(BW, G, stride=2), :] = pltpu.roll(even, NS, 1)
    wide[pl.ds(BW + 1, G, stride=2), :] = odd


def products(rows, a_nat, w_ref, place_s, slot_of, accs):
    for k in range(KN):
        for i, acc in zip(rows, accs):
            block = a_nat[k, pl.ds(i, G, stride=STEP), :].astype(jnp.bfloat16)
            place = place_s[k, i]
            slot = slot_of(place, i)
            acc[slot] += jnp.dot(block, w_ref[place], preferred_element_type=jnp.float32)


def onto_coarse(groups, accs, sels):
    sums = {}
    low = low_lanes(NS)
    for at, group in enumerate(groups):
        first, count = IDS[group]
        mine = accs[at * 8:at * 8 + 8]
        rows = [jnp.concatenate([acc[s] for s in range(SL)], axis=1).astype(jnp.bfloat16) for acc in mine]
        full = lax.dot_general(jnp.concatenate(rows, axis=0), sels[at][...], (((0,), (0,)), ((), ())),
                               preferred_element_type=jnp.float32)
        for c in range(count):
            cc = full[:, c * 128:(c + 1) * 128]
            part = lambda s, par: cc[s * 128 + par * NS:s * 128 + (par + 1) * NS]
            for pair in range(3):
                s0, s1 = 2 * pair, min(2 * pair + 1, SL - 1)
                stay = jnp.where(low, part(s0, 0), part(s1, 1))
                move = jnp.where(low, part(s1, 0), part(s0, 1))
                both = stay + pltpu.roll(move, NS, 1)
                key = (first + c, pair)
                sums[key] = sums[key] + both if key in sums else both
    return sums


def inner_kernel(place_v, agg_v, p_ref, a_ref, a_nat, w_ref, sel_a, sel_d, part_ref, *scratch):
    p_nat, wide, sel_b, sel_c, place_s, agg_s, glob, sems = scratch[:8]
    accs = scratch[8:]
    place_in = pltpu.make_async_copy(place_v, place_s, sems.at[0])
    agg_in = pltpu.make_async_copy(agg_v, agg_s, sems.at[1])
    place_in.start()
    agg_in.start()
    for acc in accs:
        acc[...] = jnp.zeros_like(acc)
    sels = (sel_a, sel_b, sel_c, sel_d)
    for sel in sels:
        sel[...] = jnp.zeros_like(sel)
    for h in range(G):
        p_nat[pl.ds(h * STEP, NB), :] = p_ref[:, pl.ds(h * 128, 128)].astype(jnp.float32)
    place_in.wait()
    agg_in.wait()
    for t in range(NB):
        glob[t] = agg_s[t]
    glob[NONE] = 1
    low = low_lanes(G)
    for j in range(NB):
        nat = p_nat[pl.ds(j, G, stride=STEP), :]
        widen(nat, wide.at[j], low)
        w_ref[j] = wide[j].astype(jnp.bfloat16)
        lane = pl.multiple_of((agg_s[j] - IDS[j // 8][0]) * 128, 128)
        sels[j // 8][pl.ds(j % 8 * G, G), pl.ds(lane, 128)] = nat.astype(jnp.bfloat16)
    w_ref[NONE] = jnp.zeros((128, 128), jnp.bfloat16)
    for k in range(KN):
        for g in range(G):
            a_nat[k, pl.ds(g * STEP, NB), :] = a_ref[:, pl.ds(k * BLK + g * 128, 128)].astype(jnp.float32)

    products(INNER, a_nat, w_ref, place_s, lambda place, i: glob[place] - agg_s[i] + RC, accs)
    for (c, pair), value in onto_coarse((1, 2), accs, (sel_b, sel_c)).items():
        part_ref[:, pl.ds(c * 8, 8), pl.ds(pair * 128, 128)] = value.reshape(8, 8, 128)


def outer_kernel(place_v, agg_v, hi_ref, lo_ref, a_nat, w_own, sel_a, sel_d, part_ref, out_ref, *scratch):
    p_nat, wide, w_all, place_s, agg_s, glob, sems = scratch[:7]
    accs = scratch[7:]
    place_in = pltpu.make_async_copy(place_v, place_s, sems.at[0])
    agg_in = pltpu.make_async_copy(agg_v, agg_s, sems.at[1])
    place_in.start()
    agg_in.start()
    below = jnp.max(lo_ref[:, BLK:].astype(jnp.float32)).astype(jnp.int32)
    above = jnp.max(hi_ref[:, BLK:].astype(jnp.float32)).astype(jnp.int32)
    for acc in accs:
        acc[...] = jnp.zeros_like(acc)
    for h in range(G):
        lanes = pl.ds(h * 128, 128)
        p_nat[pl.ds(h * HALO_STEP, HW), :] = lo_ref[:, lanes].astype(jnp.float32)
        p_nat[pl.ds(h * HALO_STEP + HW, HW), :] = hi_ref[:, lanes].astype(jnp.float32)
    w_all[:LOW] = w_own[...]
    low = low_lanes(G)
    for j in range(2 * HW):
        widen(p_nat[pl.ds(j, G, stride=HALO_STEP), :], wide.at[j], low)
        w_all[LOW + j] = wide[j].astype(jnp.bfloat16)
    place_in.wait()
    agg_in.wait()
    for t in range(NB):
        glob[t] = agg_s[t]
    glob[NONE] = 1
    for t in range(HW):
        glob[LOW + t] = jnp.where(HW - t <= below, -1, -2)
        glob[HIGH + t] = jnp.where(t < above, LA, LA + 1)
    products(OUTER, a_nat, w_all, place_s, lambda place, i: glob[place] - agg_s[i] + RC, accs)
    sums = onto_coarse((0, 3), accs, (sel_a, sel_d))
    for c in range(0, LA, 2):
        for pair in range(3):
            lanes = min(128, SL * NS - pair * 128)
            both = jnp.concatenate([sums[c, pair].reshape(8, 8, 128), sums[c + 1, pair].reshape(8, 8, 128)], axis=1)
            both = both + part_ref[:, pl.ds(c * 8, 16), pl.ds(pair * 128, 128)]
            out_ref[:, pl.ds(c * 8, 16), pl.ds(pair * 128, lanes)] = both[:, :, :lanes].astype(jnp.bfloat16)


def load(prolong, aggregate, columns_t, a_blocks):
    halo = shape((HW, BLK + 128), jnp.bfloat16)
    return pl.pallas_call(
        load_kernel,
        out_shape=(halo, halo, shape((KN, NB), jnp.int32), shape((NB,), jnp.int32), shape((NB, BLK), jnp.bfloat16),
                   shape((NB, KN * BLK), jnp.bfloat16)),
        in_specs=[HBM] * 4,
        out_specs=[VMEM] * 6,
        scratch_shapes=[pltpu.SMEM((NB,), jnp.int32), pltpu.SemaphoreType.DMA((5,))],
        compiler_params=SMALL,
    )(*(pltpu.with_memory_space_constraint(x, pltpu.HBM) for x in (prolong, aggregate, columns_t, a_blocks)))


def sel_shape(group):
    return 8 * G, IDS[group][1] * 128


def inner(place, agg, p_v, a_v):
    return pl.pallas_call(
        inner_kernel,
        out_shape=(shape((KN, G * STEP, 128), jnp.float32), shape((LOW, 128, 128), jnp.bfloat16),
                   shape(sel_shape(0), jnp.bfloat16), shape(sel_shape(3), jnp.bfloat16),
                   shape((COLS, LA * NS // COLS, 3 * 128), jnp.float32)),
        in_specs=[VMEM] * 4,
        out_specs=[VMEM] * 5,
        scratch_shapes=[
            pltpu.VMEM((G * STEP, 128), jnp.float32),
            pltpu.VMEM((NB, 128, 128), jnp.float32),
            pltpu.VMEM(sel_shape(1), jnp.bfloat16),
            pltpu.VMEM(sel_shape(2), jnp.bfloat16),
            pltpu.SMEM((KN, NB), jnp.int32),
            pltpu.SMEM((NB,), jnp.int32),
            pltpu.SMEM((PLACES,), jnp.int32),
            pltpu.SemaphoreType.DMA((2,)),
        ] + [pltpu.VMEM((SL, G, 128), jnp.float32)] * len(INNER),
        compiler_params=SMALL,
    )(place, agg, p_v, a_v)


def outer(place, agg, hi, lo, *mid):
    return pl.pallas_call(
        outer_kernel,
        out_shape=shape((COLS, LA * NS // COLS, SL * NS), jnp.bfloat16),
        in_specs=[VMEM] * 9,
        out_specs=VMEM,
        scratch_shapes=[
            pltpu.VMEM((G * HALO_STEP, 128), jnp.float32),
            pltpu.VMEM((2 * HW, 128, 128), jnp.float32),
            pltpu.VMEM((PLACES, 128, 128), jnp.bfloat16),
            pltpu.SMEM((KN, NB), jnp.int32),
            pltpu.SMEM((NB,), jnp.int32),
            pltpu.SMEM((PLACES,), jnp.int32),
            pltpu.SemaphoreType.DMA((2,)),
        ] + [pltpu.VMEM((SL, G, 128), jnp.float32)] * len(OUTER),
        compiler_params=SMALL,
    )(place, agg, hi, lo, *mid)


def shifted(shard, by):
    axis = ("rows", "cols")
    length = lax.axis_size(axis)
    return lax.ppermute(shard, axis, [(i, (i + by) % length) for i in range(length)])


def shards(a_blocks, prolong, columns, aggregate):
    down, up, place, agg, p_v, a_v = load(prolong, aggregate, columns.T, a_blocks)
    hi = shifted(down, -1)
    lo = shifted(up, 1)
    mid = inner(place, agg, p_v, a_v)
    mine = outer(place, agg, hi, lo, *mid)
    landed = lax.all_to_all(mine, "cols", split_axis=0, concat_axis=0, tiled=True)
    return landed.astype(jnp.float32).reshape(COLS * LA, NS // COLS, SL * NS)


def solution(mesh):
    in_specs = (
        P(("rows", "cols"), None),
        P(("rows", "cols"), None),
        P(("rows", "cols"), None),
        P(("rows", "cols")),
    )
    out_specs = P("rows", "cols", None)
    return jax.shard_map(shards, mesh=mesh, in_specs=in_specs, out_specs=out_specs, check_vma=False)
```

```python
import jax
import jax.numpy as jnp
from jax import lax
from jax.experimental import pallas as pl
from jax.experimental.pallas import tpu as pltpu
from jax.sharding import PartitionSpec as P

BW = 64
NS = 64
KN = 7
HW = 8
RC = 2
SL = 5
LA = 4
NB = 32
G = BW // 2
BLK = BW * BW
COLS = 8
NONE = NB
LOW = NB + 1
HIGH = LOW + HW
PLACES = HIGH + HW
STEP = NB + 8
HALO_STEP = 2 * HW + 8
IDS = ((0, 2), (0, 3), (1, 3), (2, 2))
INNER = tuple(range(HW, NB - HW))
OUTER = tuple(range(HW)) + tuple(range(NB - HW, NB))

VMEM = pl.BlockSpec(memory_space=pltpu.VMEM)
HBM = pl.BlockSpec(memory_space=pltpu.HBM)
SMALL = pltpu.CompilerParams(vmem_limit_bytes=24 * 1024 * 1024)


def shape(dims, dtype):
    return jax.ShapeDtypeStruct(dims, dtype)


def low_lanes(rows):
    return lax.broadcasted_iota(jnp.int32, (rows, 128), 1) < NS


def is_even():
    return jnp.bitwise_and(lax.axis_index("cols"), 1) == 0


def load_kernel(p_hbm, agg_hbm, cols_hbm, a_hbm, first_ref, second_ref, place_ref, agg_ref, p_ref, a_ref, agg_s, sems):
    p_in = pltpu.make_async_copy(p_hbm, p_ref, sems.at[0])
    ids_in = pltpu.make_async_copy(agg_hbm, agg_s, sems.at[1])
    cols_in = pltpu.make_async_copy(cols_hbm, place_ref, sems.at[2])
    agg_in = pltpu.make_async_copy(agg_hbm, agg_ref, sems.at[3])
    a_in = pltpu.make_async_copy(a_hbm, a_ref, sems.at[4])
    for c in (p_in, ids_in, cols_in, agg_in, a_in):
        c.start()
    ids_in.wait()
    last, first = jnp.int32(0), jnp.int32(0)
    for t in range(HW):
        last += (agg_s[NB - HW + t] == LA - 1).astype(jnp.int32)
        first += (agg_s[t] == 0).astype(jnp.int32)
    cols_in.wait()
    cols = place_ref[...]
    row = lax.broadcasted_iota(jnp.int32, cols.shape, 1)
    rel = row + jnp.bitwise_and(cols - row + HW, NB - 1) - HW
    place = jnp.where(rel < 0, rel + HW + LOW, jnp.where(rel < NB, rel, rel - NB + HIGH))
    place_ref[...] = jnp.where(cols < 0, NONE, place)
    p_in.wait()
    even = is_even()

    def fill(up_ref, down_ref):
        up_ref[:, :BLK] = p_ref[NB - HW:, :]
        up_ref[:, BLK:] = jnp.full((HW, 128), last.astype(jnp.float32), jnp.float32).astype(jnp.bfloat16)
        down_ref[:, :BLK] = p_ref[:HW, :]
        down_ref[:, BLK:] = jnp.full((HW, 128), first.astype(jnp.float32), jnp.float32).astype(jnp.bfloat16)

    pl.when(even)(lambda: fill(first_ref, second_ref))
    pl.when(jnp.logical_not(even))(lambda: fill(second_ref, first_ref))
    agg_in.wait()
    a_in.wait()


def widen(nat, wide, low):
    even = jnp.where(low, nat, 0.0)
    odd = jnp.where(low, 0.0, nat)
    wide[pl.ds(0, G, stride=2), :] = even
    wide[pl.ds(1, G, stride=2), :] = pltpu.roll(odd, NS, 1)
    wide[pl.ds(BW, G, stride=2), :] = pltpu.roll(even, NS, 1)
    wide[pl.ds(BW + 1, G, stride=2), :] = odd


def products(rows, a_nat, w_ref, place_s, slot_of, accs):
    for k in range(KN):
        for i, acc in zip(rows, accs):
            block = a_nat[k, pl.ds(i, G, stride=STEP), :].astype(jnp.bfloat16)
            place = place_s[k, i]
            slot = slot_of(place, i)
            acc[slot] += jnp.dot(block, w_ref[place], preferred_element_type=jnp.float32)


def onto_coarse(groups, accs, sels):
    sums = {}
    low = low_lanes(NS)
    for at, group in enumerate(groups):
        first, count = IDS[group]
        mine = accs[at * 8:at * 8 + 8]
        rows = [jnp.concatenate([acc[s] for s in range(SL)], axis=1).astype(jnp.bfloat16) for acc in mine]
        full = lax.dot_general(jnp.concatenate(rows, axis=0), sels[at][...], (((0,), (0,)), ((), ())),
                               preferred_element_type=jnp.float32)
        for c in range(count):
            cc = full[:, c * 128:(c + 1) * 128]
            part = lambda s, par: cc[s * 128 + par * NS:s * 128 + (par + 1) * NS]
            for pair in range(3):
                s0, s1 = 2 * pair, min(2 * pair + 1, SL - 1)
                stay = jnp.where(low, part(s0, 0), part(s1, 1))
                move = jnp.where(low, part(s1, 0), part(s0, 1))
                both = stay + pltpu.roll(move, NS, 1)
                key = (first + c, pair)
                sums[key] = sums[key] + both if key in sums else both
    return sums


def inner_kernel(place_v, agg_v, p_ref, a_ref, a_nat, w_ref, sel_a, sel_d, part_ref, *scratch):
    p_nat, wide, sel_b, sel_c, place_s, agg_s, glob, sems = scratch[:8]
    accs = scratch[8:]
    place_in = pltpu.make_async_copy(place_v, place_s, sems.at[0])
    agg_in = pltpu.make_async_copy(agg_v, agg_s, sems.at[1])
    place_in.start()
    agg_in.start()
    for acc in accs:
        acc[...] = jnp.zeros_like(acc)
    sels = (sel_a, sel_b, sel_c, sel_d)
    for sel in sels:
        sel[...] = jnp.zeros_like(sel)
    for h in range(G):
        p_nat[pl.ds(h * STEP, NB), :] = p_ref[:, pl.ds(h * 128, 128)].astype(jnp.float32)
    place_in.wait()
    agg_in.wait()
    for t in range(NB):
        glob[t] = agg_s[t]
    glob[NONE] = 1
    low = low_lanes(G)
    for j in range(NB):
        nat = p_nat[pl.ds(j, G, stride=STEP), :]
        widen(nat, wide.at[j], low)
        w_ref[j] = wide[j].astype(jnp.bfloat16)
        lane = pl.multiple_of((agg_s[j] - IDS[j // 8][0]) * 128, 128)
        sels[j // 8][pl.ds(j % 8 * G, G), pl.ds(lane, 128)] = nat.astype(jnp.bfloat16)
    w_ref[NONE] = jnp.zeros((128, 128), jnp.bfloat16)
    for k in range(KN):
        for g in range(G):
            a_nat[k, pl.ds(g * STEP, NB), :] = a_ref[:, pl.ds(k * BLK + g * 128, 128)].astype(jnp.float32)

    products(INNER, a_nat, w_ref, place_s, lambda place, i: glob[place] - agg_s[i] + RC, accs)
    for (c, pair), value in onto_coarse((1, 2), accs, (sel_b, sel_c)).items():
        part_ref[:, pl.ds(c * 8, 8), pl.ds(pair * 128, 128)] = value.reshape(8, 8, 128)


def outer_kernel(place_v, agg_v, first_ref, second_ref, a_nat, w_own, sel_a, sel_d, part_ref, out_ref, *scratch):
    p_nat, wide, w_all, place_s, agg_s, glob, sems = scratch[:7]
    accs = scratch[7:]
    place_in = pltpu.make_async_copy(place_v, place_s, sems.at[0])
    agg_in = pltpu.make_async_copy(agg_v, agg_s, sems.at[1])
    place_in.start()
    agg_in.start()
    even = is_even()
    in_first = jnp.max(first_ref[:, BLK:].astype(jnp.float32)).astype(jnp.int32)
    in_second = jnp.max(second_ref[:, BLK:].astype(jnp.float32)).astype(jnp.int32)
    below = jnp.where(even, in_second, in_first)
    above = jnp.where(even, in_first, in_second)
    at_first = pl.multiple_of(jnp.where(even, HW, 0), HW)
    at_second = pl.multiple_of(jnp.where(even, 0, HW), HW)
    for acc in accs:
        acc[...] = jnp.zeros_like(acc)
    for h in range(G):
        lanes = pl.ds(h * 128, 128)
        p_nat[pl.ds(h * HALO_STEP + at_first, HW), :] = first_ref[:, lanes].astype(jnp.float32)
        p_nat[pl.ds(h * HALO_STEP + at_second, HW), :] = second_ref[:, lanes].astype(jnp.float32)
    w_all[:LOW] = w_own[...]
    low = low_lanes(G)
    for j in range(2 * HW):
        widen(p_nat[pl.ds(j, G, stride=HALO_STEP), :], wide.at[j], low)
        w_all[LOW + j] = wide[j].astype(jnp.bfloat16)
    place_in.wait()
    agg_in.wait()
    for t in range(NB):
        glob[t] = agg_s[t]
    glob[NONE] = 1
    for t in range(HW):
        glob[LOW + t] = jnp.where(HW - t <= below, -1, -2)
        glob[HIGH + t] = jnp.where(t < above, LA, LA + 1)
    products(OUTER, a_nat, w_all, place_s, lambda place, i: glob[place] - agg_s[i] + RC, accs)
    sums = onto_coarse((0, 3), accs, (sel_a, sel_d))
    for c in range(0, LA, 2):
        for pair in range(3):
            lanes = min(128, SL * NS - pair * 128)
            both = jnp.concatenate([sums[c, pair].reshape(8, 8, 128), sums[c + 1, pair].reshape(8, 8, 128)], axis=1)
            both = both + part_ref[:, pl.ds(c * 8, 16), pl.ds(pair * 128, 128)]
            out_ref[:, pl.ds(c * 8, 16), pl.ds(pair * 128, lanes)] = both[:, :, :lanes].astype(jnp.bfloat16)


def load(prolong, aggregate, columns_t, a_blocks):
    halo = shape((HW, BLK + 128), jnp.bfloat16)
    return pl.pallas_call(
        load_kernel,
        out_shape=(halo, halo, shape((KN, NB), jnp.int32), shape((NB,), jnp.int32), shape((NB, BLK), jnp.bfloat16),
                   shape((NB, KN * BLK), jnp.bfloat16)),
        in_specs=[HBM] * 4,
        out_specs=[VMEM] * 6,
        scratch_shapes=[pltpu.SMEM((NB,), jnp.int32), pltpu.SemaphoreType.DMA((5,))],
        compiler_params=SMALL,
    )(*(pltpu.with_memory_space_constraint(x, pltpu.HBM) for x in (prolong, aggregate, columns_t, a_blocks)))


def sel_shape(group):
    return 8 * G, IDS[group][1] * 128


def inner(place, agg, p_v, a_v):
    return pl.pallas_call(
        inner_kernel,
        out_shape=(shape((KN, G * STEP, 128), jnp.float32), shape((LOW, 128, 128), jnp.bfloat16),
                   shape(sel_shape(0), jnp.bfloat16), shape(sel_shape(3), jnp.bfloat16),
                   shape((COLS, LA * NS // COLS, 3 * 128), jnp.float32)),
        in_specs=[VMEM] * 4,
        out_specs=[VMEM] * 5,
        scratch_shapes=[
            pltpu.VMEM((G * STEP, 128), jnp.float32),
            pltpu.VMEM((NB, 128, 128), jnp.float32),
            pltpu.VMEM(sel_shape(1), jnp.bfloat16),
            pltpu.VMEM(sel_shape(2), jnp.bfloat16),
            pltpu.SMEM((KN, NB), jnp.int32),
            pltpu.SMEM((NB,), jnp.int32),
            pltpu.SMEM((PLACES,), jnp.int32),
            pltpu.SemaphoreType.DMA((2,)),
        ] + [pltpu.VMEM((SL, G, 128), jnp.float32)] * len(INNER),
        compiler_params=SMALL,
    )(place, agg, p_v, a_v)


def outer(place, agg, first, second, *mid):
    return pl.pallas_call(
        outer_kernel,
        out_shape=shape((COLS, LA * NS // COLS, SL * NS), jnp.bfloat16),
        in_specs=[VMEM] * 9,
        out_specs=VMEM,
        scratch_shapes=[
            pltpu.VMEM((G * HALO_STEP, 128), jnp.float32),
            pltpu.VMEM((2 * HW, 128, 128), jnp.float32),
            pltpu.VMEM((PLACES, 128, 128), jnp.bfloat16),
            pltpu.SMEM((KN, NB), jnp.int32),
            pltpu.SMEM((NB,), jnp.int32),
            pltpu.SMEM((PLACES,), jnp.int32),
            pltpu.SemaphoreType.DMA((2,)),
        ] + [pltpu.VMEM((SL, G, 128), jnp.float32)] * len(OUTER),
        compiler_params=SMALL,
    )(place, agg, first, second, *mid)


def exchanged(shard, first):
    axis = ("rows", "cols")
    length = lax.axis_size(axis)
    pairs = [(i, (i + (1 if (i % 2 == 0) == first else -1)) % length) for i in range(length)]
    return lax.ppermute(shard, axis, pairs)


def shards(a_blocks, prolong, columns, aggregate):
    first, second, place, agg, p_v, a_v = load(prolong, aggregate, columns.T, a_blocks)
    first = exchanged(first, True)
    second = exchanged(second, False)
    mid = inner(place, agg, p_v, a_v)
    mine = outer(place, agg, first, second, *mid)
    landed = lax.all_to_all(mine, "cols", split_axis=0, concat_axis=0, tiled=True)
    return landed.astype(jnp.float32).reshape(COLS * LA, NS // COLS, SL * NS)


def solution(mesh):
    in_specs = (
        P(("rows", "cols"), None),
        P(("rows", "cols"), None),
        P(("rows", "cols"), None),
        P(("rows", "cols")),
    )
    out_specs = P("rows", "cols", None)
    return jax.shard_map(shards, mesh=mesh, in_specs=in_specs, out_specs=out_specs, check_vma=False)
```

```python
import jax
import jax.numpy as jnp
from jax import lax
from jax.experimental import pallas as pl
from jax.experimental.pallas import tpu as pltpu
from jax.sharding import PartitionSpec as P

BW = 64
NS = 64
KN = 7
HW = 8
RC = 2
SL = 5
LA = 4
NB = 32
G = BW // 2
BLK = BW * BW
COLS = 8
NONE = NB
LOW = NB + 1
HIGH = LOW + HW
PLACES = HIGH + HW
STEP = NB + 8
HALO_STEP = 2 * HW + 8
IDS = ((0, 2), (0, 3), (1, 3), (2, 2))
INNER = tuple(range(HW, NB - HW))
OUTER = tuple(range(HW)) + tuple(range(NB - HW, NB))

VMEM = pl.BlockSpec(memory_space=pltpu.VMEM)
HBM = pl.BlockSpec(memory_space=pltpu.HBM)
SMALL = pltpu.CompilerParams(vmem_limit_bytes=24 * 1024 * 1024)


def shape(dims, dtype):
    return jax.ShapeDtypeStruct(dims, dtype)


def low_lanes(rows):
    return lax.broadcasted_iota(jnp.int32, (rows, 128), 1) < NS


def above_first():
    return jnp.bitwise_and(lax.axis_index("cols"), 1) == 1


def load_kernel(p_hbm, agg_hbm, cols_hbm, first_ref, second_ref, place_ref, agg_ref, p_ref, agg_s, sems):
    p_in = pltpu.make_async_copy(p_hbm, p_ref, sems.at[0])
    ids_in = pltpu.make_async_copy(agg_hbm, agg_s, sems.at[1])
    cols_in = pltpu.make_async_copy(cols_hbm, place_ref, sems.at[2])
    agg_in = pltpu.make_async_copy(agg_hbm, agg_ref, sems.at[3])
    for c in (p_in, ids_in, cols_in, agg_in):
        c.start()
    ids_in.wait()
    last, first = jnp.int32(0), jnp.int32(0)
    for t in range(HW):
        last += (agg_s[NB - HW + t] == LA - 1).astype(jnp.int32)
        first += (agg_s[t] == 0).astype(jnp.int32)
    cols_in.wait()
    cols = place_ref[...]
    row = lax.broadcasted_iota(jnp.int32, cols.shape, 1)
    rel = row + jnp.bitwise_and(cols - row + HW, NB - 1) - HW
    place = jnp.where(rel < 0, rel + HW + LOW, jnp.where(rel < NB, rel, rel - NB + HIGH))
    place_ref[...] = jnp.where(cols < 0, NONE, place)
    p_in.wait()
    up_first = above_first()

    def fill(up_ref, down_ref):
        up_ref[:, :BLK] = p_ref[NB - HW:, :]
        up_ref[:, BLK:] = jnp.full((HW, 128), last.astype(jnp.float32), jnp.float32).astype(jnp.bfloat16)
        down_ref[:, :BLK] = p_ref[:HW, :]
        down_ref[:, BLK:] = jnp.full((HW, 128), first.astype(jnp.float32), jnp.float32).astype(jnp.bfloat16)

    pl.when(up_first)(lambda: fill(first_ref, second_ref))
    pl.when(jnp.logical_not(up_first))(lambda: fill(second_ref, first_ref))
    agg_in.wait()


def widen(nat, wide, low):
    even = jnp.where(low, nat, 0.0)
    odd = jnp.where(low, 0.0, nat)
    wide[pl.ds(0, G, stride=2), :] = even
    wide[pl.ds(1, G, stride=2), :] = pltpu.roll(odd, NS, 1)
    wide[pl.ds(BW, G, stride=2), :] = pltpu.roll(even, NS, 1)
    wide[pl.ds(BW + 1, G, stride=2), :] = odd


def products(rows, a_nat, w_ref, place_s, slot_of, accs):
    for k in range(KN):
        for i, acc in zip(rows, accs):
            block = a_nat[k, pl.ds(i, G, stride=STEP), :].astype(jnp.bfloat16)
            place = place_s[k, i]
            slot = slot_of(place, i)
            acc[slot] += jnp.dot(block, w_ref[place], preferred_element_type=jnp.float32)


def onto_coarse(groups, accs, sels):
    sums = {}
    low = low_lanes(NS)
    for at, group in enumerate(groups):
        first, count = IDS[group]
        mine = accs[at * 8:at * 8 + 8]
        rows = [jnp.concatenate([acc[s] for s in range(SL)], axis=1).astype(jnp.bfloat16) for acc in mine]
        full = lax.dot_general(jnp.concatenate(rows, axis=0), sels[at][...], (((0,), (0,)), ((), ())),
                               preferred_element_type=jnp.float32)
        for c in range(count):
            cc = full[:, c * 128:(c + 1) * 128]
            part = lambda s, par: cc[s * 128 + par * NS:s * 128 + (par + 1) * NS]
            for pair in range(3):
                s0, s1 = 2 * pair, min(2 * pair + 1, SL - 1)
                stay = jnp.where(low, part(s0, 0), part(s1, 1))
                move = jnp.where(low, part(s1, 0), part(s0, 1))
                both = stay + pltpu.roll(move, NS, 1)
                key = (first + c, pair)
                sums[key] = sums[key] + both if key in sums else both
    return sums


def inner_kernel(place_v, agg_v, p_ref, a_hbm, a_nat, w_ref, sel_a, sel_d, part_ref, *scratch):
    a_ref, p_nat, wide, sel_b, sel_c, place_s, agg_s, glob, sems = scratch[:9]
    accs = scratch[9:]
    a_in = []
    for k in range(KN):
        part = (slice(None), pl.ds(k * BLK, BLK))
        a_in.append(pltpu.make_async_copy(a_hbm.at[part], a_ref.at[part], sems.at[2 + k]))
        a_in[k].start()
    place_in = pltpu.make_async_copy(place_v, place_s, sems.at[0])
    agg_in = pltpu.make_async_copy(agg_v, agg_s, sems.at[1])
    place_in.start()
    agg_in.start()
    for acc in accs:
        acc[...] = jnp.zeros_like(acc)
    sels = (sel_a, sel_b, sel_c, sel_d)
    for sel in sels:
        sel[...] = jnp.zeros_like(sel)
    for h in range(G):
        p_nat[pl.ds(h * STEP, NB), :] = p_ref[:, pl.ds(h * 128, 128)].astype(jnp.float32)
    place_in.wait()
    agg_in.wait()
    for t in range(NB):
        glob[t] = agg_s[t]
    glob[NONE] = 1
    low = low_lanes(G)
    for j in range(NB):
        nat = p_nat[pl.ds(j, G, stride=STEP), :]
        widen(nat, wide.at[j], low)
        w_ref[j] = wide[j].astype(jnp.bfloat16)
        lane = pl.multiple_of((agg_s[j] - IDS[j // 8][0]) * 128, 128)
        sels[j // 8][pl.ds(j % 8 * G, G), pl.ds(lane, 128)] = nat.astype(jnp.bfloat16)
    w_ref[NONE] = jnp.zeros((128, 128), jnp.bfloat16)
    for k in range(KN):
        a_in[k].wait()
        for g in range(G):
            a_nat[k, pl.ds(g * STEP, NB), :] = a_ref[:, pl.ds(k * BLK + g * 128, 128)].astype(jnp.float32)

    products(INNER, a_nat, w_ref, place_s, lambda place, i: glob[place] - agg_s[i] + RC, accs)
    for (c, pair), value in onto_coarse((1, 2), accs, (sel_b, sel_c)).items():
        part_ref[:, pl.ds(c * 8, 8), pl.ds(pair * 128, 128)] = value.reshape(8, 8, 128)


def outer_kernel(place_v, agg_v, first_ref, second_ref, a_nat, w_own, sel_a, sel_d, part_ref, out_ref, *scratch):
    p_nat, wide, w_all, place_s, agg_s, glob, sems = scratch[:7]
    accs = scratch[7:]
    place_in = pltpu.make_async_copy(place_v, place_s, sems.at[0])
    agg_in = pltpu.make_async_copy(agg_v, agg_s, sems.at[1])
    place_in.start()
    agg_in.start()
    up_first = above_first()
    in_first = jnp.max(first_ref[:, BLK:].astype(jnp.float32)).astype(jnp.int32)
    in_second = jnp.max(second_ref[:, BLK:].astype(jnp.float32)).astype(jnp.int32)
    below = jnp.where(up_first, in_second, in_first)
    above = jnp.where(up_first, in_first, in_second)
    at_first = pl.multiple_of(jnp.where(up_first, HW, 0), HW)
    at_second = pl.multiple_of(jnp.where(up_first, 0, HW), HW)
    for acc in accs:
        acc[...] = jnp.zeros_like(acc)
    for h in range(G):
        lanes = pl.ds(h * 128, 128)
        p_nat[pl.ds(h * HALO_STEP + at_first, HW), :] = first_ref[:, lanes].astype(jnp.float32)
        p_nat[pl.ds(h * HALO_STEP + at_second, HW), :] = second_ref[:, lanes].astype(jnp.float32)
    w_all[:LOW] = w_own[...]
    low = low_lanes(G)
    for j in range(2 * HW):
        widen(p_nat[pl.ds(j, G, stride=HALO_STEP), :], wide.at[j], low)
        w_all[LOW + j] = wide[j].astype(jnp.bfloat16)
    place_in.wait()
    agg_in.wait()
    for t in range(NB):
        glob[t] = agg_s[t]
    glob[NONE] = 1
    for t in range(HW):
        glob[LOW + t] = jnp.where(HW - t <= below, -1, -2)
        glob[HIGH + t] = jnp.where(t < above, LA, LA + 1)
    products(OUTER, a_nat, w_all, place_s, lambda place, i: glob[place] - agg_s[i] + RC, accs)
    sums = onto_coarse((0, 3), accs, (sel_a, sel_d))
    for c in range(0, LA, 2):
        for pair in range(3):
            lanes = min(128, SL * NS - pair * 128)
            both = jnp.concatenate([sums[c, pair].reshape(8, 8, 128), sums[c + 1, pair].reshape(8, 8, 128)], axis=1)
            both = both + part_ref[:, pl.ds(c * 8, 16), pl.ds(pair * 128, 128)]
            out_ref[:, pl.ds(c * 8, 16), pl.ds(pair * 128, lanes)] = both[:, :, :lanes].astype(jnp.bfloat16)


def load(prolong, aggregate, columns_t):
    halo = shape((HW, BLK + 128), jnp.bfloat16)
    return pl.pallas_call(
        load_kernel,
        out_shape=(halo, halo, shape((KN, NB), jnp.int32), shape((NB,), jnp.int32), shape((NB, BLK), jnp.bfloat16)),
        in_specs=[HBM] * 3,
        out_specs=[VMEM] * 5,
        scratch_shapes=[pltpu.SMEM((NB,), jnp.int32), pltpu.SemaphoreType.DMA((4,))],
        compiler_params=SMALL,
    )(*(pltpu.with_memory_space_constraint(x, pltpu.HBM) for x in (prolong, aggregate, columns_t)))


def sel_shape(group):
    return 8 * G, IDS[group][1] * 128


def inner(place, agg, p_v, a_blocks):
    return pl.pallas_call(
        inner_kernel,
        out_shape=(shape((KN, G * STEP, 128), jnp.float32), shape((LOW, 128, 128), jnp.bfloat16),
                   shape(sel_shape(0), jnp.bfloat16), shape(sel_shape(3), jnp.bfloat16),
                   shape((COLS, LA * NS // COLS, 3 * 128), jnp.float32)),
        in_specs=[VMEM] * 3 + [HBM],
        out_specs=[VMEM] * 5,
        scratch_shapes=[
            pltpu.VMEM((NB, KN * BLK), jnp.bfloat16),
            pltpu.VMEM((G * STEP, 128), jnp.float32),
            pltpu.VMEM((NB, 128, 128), jnp.float32),
            pltpu.VMEM(sel_shape(1), jnp.bfloat16),
            pltpu.VMEM(sel_shape(2), jnp.bfloat16),
            pltpu.SMEM((KN, NB), jnp.int32),
            pltpu.SMEM((NB,), jnp.int32),
            pltpu.SMEM((PLACES,), jnp.int32),
            pltpu.SemaphoreType.DMA((2 + KN,)),
        ] + [pltpu.VMEM((SL, G, 128), jnp.float32)] * len(INNER),
        compiler_params=SMALL,
    )(place, agg, p_v, pltpu.with_memory_space_constraint(a_blocks, pltpu.HBM))


def outer(place, agg, first, second, *mid):
    return pl.pallas_call(
        outer_kernel,
        out_shape=shape((COLS, LA * NS // COLS, SL * NS), jnp.bfloat16),
        in_specs=[VMEM] * 9,
        out_specs=VMEM,
        scratch_shapes=[
            pltpu.VMEM((G * HALO_STEP, 128), jnp.float32),
            pltpu.VMEM((2 * HW, 128, 128), jnp.float32),
            pltpu.VMEM((PLACES, 128, 128), jnp.bfloat16),
            pltpu.SMEM((KN, NB), jnp.int32),
            pltpu.SMEM((NB,), jnp.int32),
            pltpu.SMEM((PLACES,), jnp.int32),
            pltpu.SemaphoreType.DMA((2,)),
        ] + [pltpu.VMEM((SL, G, 128), jnp.float32)] * len(OUTER),
        compiler_params=SMALL,
    )(place, agg, first, second, *mid)


def exchanged(shard, first):
    axis = ("rows", "cols")
    length = lax.axis_size(axis)
    pairs = [(i, (i + (1 if (i % 2 == 1) == first else -1)) % length) for i in range(length)]
    return lax.ppermute(shard, axis, pairs)


def shards(a_blocks, prolong, columns, aggregate):
    first, second, place, agg, p_v = load(prolong, aggregate, columns.T)
    first = exchanged(first, True)
    second = exchanged(second, False)
    mid = inner(place, agg, p_v, a_blocks)
    mine = outer(place, agg, first, second, *mid)
    landed = lax.all_to_all(mine, "cols", split_axis=0, concat_axis=0, tiled=True)
    return landed.astype(jnp.float32).reshape(COLS * LA, NS // COLS, SL * NS)


def solution(mesh):
    in_specs = (
        P(("rows", "cols"), None),
        P(("rows", "cols"), None),
        P(("rows", "cols"), None),
        P(("rows", "cols")),
    )
    out_specs = P("rows", "cols", None)
    return jax.shard_map(shards, mesh=mesh, in_specs=in_specs, out_specs=out_specs, check_vma=False)
```

```python
import jax
import jax.numpy as jnp
from jax import lax
from jax.experimental import pallas as pl
from jax.experimental.pallas import tpu as pltpu
from jax.sharding import PartitionSpec as P

BW = 64
NS = 64
KN = 7
HW = 8
RC = 2
SL = 5
LA = 4
NB = 32
G = BW // 2
BLK = BW * BW
COLS = 8
NONE = NB
LOW = NB + 1
HIGH = LOW + HW
PLACES = HIGH + HW
STEP = NB + 8
HALO_STEP = 2 * HW + 8
IDS = ((0, 2), (0, 3), (1, 3), (2, 2))
INNER = tuple(range(HW, NB - HW))
OUTER = tuple(range(HW)) + tuple(range(NB - HW, NB))

VMEM = pl.BlockSpec(memory_space=pltpu.VMEM)
HBM = pl.BlockSpec(memory_space=pltpu.HBM)
SMALL = pltpu.CompilerParams(vmem_limit_bytes=24 * 1024 * 1024)


def shape(dims, dtype):
    return jax.ShapeDtypeStruct(dims, dtype)


def low_lanes(rows):
    return lax.broadcasted_iota(jnp.int32, (rows, 128), 1) < NS


def above_first():
    return jnp.bitwise_and(lax.axis_index("cols"), 1) == 1


def load_kernel(p_hbm, agg_hbm, cols_hbm, first_ref, second_ref, place_ref, agg_ref, p_ref, agg_s, sems):
    p_in = pltpu.make_async_copy(p_hbm, p_ref, sems.at[0])
    ids_in = pltpu.make_async_copy(agg_hbm, agg_s, sems.at[1])
    cols_in = pltpu.make_async_copy(cols_hbm, place_ref, sems.at[2])
    agg_in = pltpu.make_async_copy(agg_hbm, agg_ref, sems.at[3])
    for c in (p_in, ids_in, cols_in, agg_in):
        c.start()
    ids_in.wait()
    last, first = jnp.int32(0), jnp.int32(0)
    for t in range(HW):
        last += (agg_s[NB - HW + t] == LA - 1).astype(jnp.int32)
        first += (agg_s[t] == 0).astype(jnp.int32)
    cols_in.wait()
    cols = place_ref[...]
    row = lax.broadcasted_iota(jnp.int32, cols.shape, 1)
    rel = row + jnp.bitwise_and(cols - row + HW, NB - 1) - HW
    place = jnp.where(rel < 0, rel + HW + LOW, jnp.where(rel < NB, rel, rel - NB + HIGH))
    place_ref[...] = jnp.where(cols < 0, NONE, place)
    p_in.wait()
    up_first = above_first()

    def fill(up_ref, down_ref):
        up_ref[:, :BLK] = p_ref[NB - HW:, :]
        up_ref[:, BLK:] = jnp.full((HW, 128), last.astype(jnp.float32), jnp.float32).astype(jnp.bfloat16)
        down_ref[:, :BLK] = p_ref[:HW, :]
        down_ref[:, BLK:] = jnp.full((HW, 128), first.astype(jnp.float32), jnp.float32).astype(jnp.bfloat16)

    pl.when(up_first)(lambda: fill(first_ref, second_ref))
    pl.when(jnp.logical_not(up_first))(lambda: fill(second_ref, first_ref))
    agg_in.wait()


def widen(nat, wide, low):
    even = jnp.where(low, nat, 0.0)
    odd = jnp.where(low, 0.0, nat)
    wide[pl.ds(0, G, stride=2), :] = even
    wide[pl.ds(1, G, stride=2), :] = pltpu.roll(odd, NS, 1)
    wide[pl.ds(BW, G, stride=2), :] = pltpu.roll(even, NS, 1)
    wide[pl.ds(BW + 1, G, stride=2), :] = odd


def products(rows, a_nat, w_ref, place_s, slot_of, accs):
    for k in range(KN):
        for i, acc in zip(rows, accs):
            block = a_nat[k, pl.ds(i, G, stride=STEP), :].astype(jnp.bfloat16)
            place = place_s[k, i]
            slot = slot_of(place, i)
            acc[slot] += jnp.dot(block, w_ref[place], preferred_element_type=jnp.float32)


def onto_coarse(groups, accs, sels):
    sums = {}
    low = low_lanes(NS)
    for at, group in enumerate(groups):
        first, count = IDS[group]
        mine = accs[at * 8:at * 8 + 8]
        rows = [jnp.concatenate([acc[s] for s in range(SL)], axis=1).astype(jnp.bfloat16) for acc in mine]
        full = lax.dot_general(jnp.concatenate(rows, axis=0), sels[at][...], (((0,), (0,)), ((), ())),
                               preferred_element_type=jnp.float32)
        for c in range(count):
            cc = full[:, c * 128:(c + 1) * 128]
            part = lambda s, par: cc[s * 128 + par * NS:s * 128 + (par + 1) * NS]
            for pair in range(3):
                s0, s1 = 2 * pair, min(2 * pair + 1, SL - 1)
                stay = jnp.where(low, part(s0, 0), part(s1, 1))
                move = jnp.where(low, part(s1, 0), part(s0, 1))
                both = stay + pltpu.roll(move, NS, 1)
                key = (first + c, pair)
                sums[key] = sums[key] + both if key in sums else both
    return sums


def inner_kernel(place_v, agg_v, p_ref, a_hbm, a_nat, w_ref, sel_a, sel_d, part_ref, *scratch):
    a_ref, p_nat, wide, sel_b, sel_c, place_s, agg_s, glob, sems = scratch[:9]
    accs = scratch[9:]
    a_in = []
    for k in range(KN):
        part = (slice(None), pl.ds(k * BLK, BLK))
        a_in.append(pltpu.make_async_copy(a_hbm.at[part], a_ref.at[part], sems.at[2 + k]))
        a_in[k].start()
    place_in = pltpu.make_async_copy(place_v, place_s, sems.at[0])
    agg_in = pltpu.make_async_copy(agg_v, agg_s, sems.at[1])
    place_in.start()
    agg_in.start()
    for acc in accs:
        acc[...] = jnp.zeros_like(acc)
    sels = (sel_a, sel_b, sel_c, sel_d)
    for sel in sels:
        sel[...] = jnp.zeros_like(sel)
    for h in range(G):
        p_nat[pl.ds(h * STEP, NB), :] = p_ref[:, pl.ds(h * 128, 128)].astype(jnp.float32)
    place_in.wait()
    agg_in.wait()
    for t in range(NB):
        glob[t] = agg_s[t]
    glob[NONE] = 1
    low = low_lanes(G)
    for j in range(NB):
        nat = p_nat[pl.ds(j, G, stride=STEP), :]
        widen(nat, wide.at[j], low)
        w_ref[j] = wide[j].astype(jnp.bfloat16)
        lane = pl.multiple_of((agg_s[j] - IDS[j // 8][0]) * 128, 128)
        sels[j // 8][pl.ds(j % 8 * G, G), pl.ds(lane, 128)] = nat.astype(jnp.bfloat16)
    w_ref[NONE] = jnp.zeros((128, 128), jnp.bfloat16)
    for k in range(KN):
        a_in[k].wait()
        for g in range(G):
            a_nat[k, pl.ds(g * STEP, NB), :] = a_ref[:, pl.ds(k * BLK + g * 128, 128)].astype(jnp.float32)

    products(INNER, a_nat, w_ref, place_s, lambda place, i: glob[place] - agg_s[i] + RC, accs)
    for (c, pair), value in onto_coarse((1, 2), accs, (sel_b, sel_c)).items():
        part_ref[:, pl.ds(c * 8, 8), pl.ds(pair * 128, 128)] = value.reshape(8, 8, 128)


def outer_kernel(place_v, agg_v, first_ref, second_ref, a_nat, w_own, sel_a, sel_d, part_ref, out_ref, *scratch):
    p_nat, wide, w_all, place_s, agg_s, glob, sems = scratch[:7]
    accs = scratch[7:]
    place_in = pltpu.make_async_copy(place_v, place_s, sems.at[0])
    agg_in = pltpu.make_async_copy(agg_v, agg_s, sems.at[1])
    place_in.start()
    agg_in.start()
    up_first = above_first()
    in_first = jnp.max(first_ref[:, BLK:].astype(jnp.float32)).astype(jnp.int32)
    in_second = jnp.max(second_ref[:, BLK:].astype(jnp.float32)).astype(jnp.int32)
    below = jnp.where(up_first, in_second, in_first)
    above = jnp.where(up_first, in_first, in_second)
    at_first = pl.multiple_of(jnp.where(up_first, HW, 0), HW)
    at_second = pl.multiple_of(jnp.where(up_first, 0, HW), HW)
    for acc in accs:
        acc[...] = jnp.zeros_like(acc)
    for h in range(G):
        lanes = pl.ds(h * 128, 128)
        p_nat[pl.ds(h * HALO_STEP + at_first, HW), :] = first_ref[:, lanes].astype(jnp.float32)
        p_nat[pl.ds(h * HALO_STEP + at_second, HW), :] = second_ref[:, lanes].astype(jnp.float32)
    w_all[:LOW] = w_own[...]
    low = low_lanes(G)
    for j in range(2 * HW):
        widen(p_nat[pl.ds(j, G, stride=HALO_STEP), :], wide.at[j], low)
        w_all[LOW + j] = wide[j].astype(jnp.bfloat16)
    place_in.wait()
    agg_in.wait()
    for t in range(NB):
        glob[t] = agg_s[t]
    glob[NONE] = 1
    for t in range(HW):
        glob[LOW + t] = jnp.where(HW - t <= below, -1, -2)
        glob[HIGH + t] = jnp.where(t < above, LA, LA + 1)
    products(OUTER, a_nat, w_all, place_s, lambda place, i: glob[place] - agg_s[i] + RC, accs)
    sums = onto_coarse((0, 3), accs, (sel_a, sel_d))
    whole = {
        (c, pair): value.reshape(8, 8, 128) + part_ref[:, pl.ds(c * 8, 8), pl.ds(pair * 128, 128)]
        for (c, pair), value in sums.items()
    }
    for c in range(LA):
        both = jnp.concatenate([whole[c, 0], whole[c, 1]], axis=1)
        out_ref[:, pl.ds(c * 16, 16), :] = both.astype(jnp.bfloat16)
    low = low_lanes(8)[None]
    tails = [jnp.where(low, whole[c, 2], whole[c + 1, 2]) for c in range(0, LA, 2)]
    out_ref[:, pl.ds(LA * 16, 16), :] = jnp.concatenate(tails, axis=1).astype(jnp.bfloat16)


def unpack_kernel(packed_ref, out_hbm, rows_ref, sems):
    copies = []
    for z in range(COLS):
        packed = packed_ref[z].astype(jnp.float32)
        for c in range(LA):
            at = z * LA + c
            rows_ref[at, :, :128] = packed[c * 16:c * 16 + 8]
            rows_ref[at, :, 128:256] = packed[c * 16 + 8:c * 16 + 16]
            tail = packed[LA * 16 + c // 2 * 8:LA * 16 + c // 2 * 8 + 8]
            rows_ref[at, :, 256:] = (tail if c % 2 == 0 else pltpu.roll(tail, NS, 1))[:, :NS]
        part = pl.ds(z * LA, LA)
        copies.append(pltpu.make_async_copy(rows_ref.at[part], out_hbm.at[part], sems.at[z]))
        copies[z].start()
    for c in copies:
        c.wait()


def load(prolong, aggregate, columns_t):
    halo = shape((HW, BLK + 128), jnp.bfloat16)
    return pl.pallas_call(
        load_kernel,
        out_shape=(halo, halo, shape((KN, NB), jnp.int32), shape((NB,), jnp.int32), shape((NB, BLK), jnp.bfloat16)),
        in_specs=[HBM] * 3,
        out_specs=[VMEM] * 5,
        scratch_shapes=[pltpu.SMEM((NB,), jnp.int32), pltpu.SemaphoreType.DMA((4,))],
        compiler_params=SMALL,
    )(*(pltpu.with_memory_space_constraint(x, pltpu.HBM) for x in (prolong, aggregate, columns_t)))


def sel_shape(group):
    return 8 * G, IDS[group][1] * 128


def inner(place, agg, p_v, a_blocks):
    return pl.pallas_call(
        inner_kernel,
        out_shape=(shape((KN, G * STEP, 128), jnp.float32), shape((LOW, 128, 128), jnp.bfloat16),
                   shape(sel_shape(0), jnp.bfloat16), shape(sel_shape(3), jnp.bfloat16),
                   shape((COLS, LA * NS // COLS, 3 * 128), jnp.float32)),
        in_specs=[VMEM] * 3 + [HBM],
        out_specs=[VMEM] * 5,
        scratch_shapes=[
            pltpu.VMEM((NB, KN * BLK), jnp.bfloat16),
            pltpu.VMEM((G * STEP, 128), jnp.float32),
            pltpu.VMEM((NB, 128, 128), jnp.float32),
            pltpu.VMEM(sel_shape(1), jnp.bfloat16),
            pltpu.VMEM(sel_shape(2), jnp.bfloat16),
            pltpu.SMEM((KN, NB), jnp.int32),
            pltpu.SMEM((NB,), jnp.int32),
            pltpu.SMEM((PLACES,), jnp.int32),
            pltpu.SemaphoreType.DMA((2 + KN,)),
        ] + [pltpu.VMEM((SL, G, 128), jnp.float32)] * len(INNER),
        compiler_params=SMALL,
    )(place, agg, p_v, pltpu.with_memory_space_constraint(a_blocks, pltpu.HBM))


def outer(place, agg, first, second, *mid):
    return pl.pallas_call(
        outer_kernel,
        out_shape=shape((COLS, LA * 16 + 16, 128), jnp.bfloat16),
        in_specs=[VMEM] * 9,
        out_specs=VMEM,
        scratch_shapes=[
            pltpu.VMEM((G * HALO_STEP, 128), jnp.float32),
            pltpu.VMEM((2 * HW, 128, 128), jnp.float32),
            pltpu.VMEM((PLACES, 128, 128), jnp.bfloat16),
            pltpu.SMEM((KN, NB), jnp.int32),
            pltpu.SMEM((NB,), jnp.int32),
            pltpu.SMEM((PLACES,), jnp.int32),
            pltpu.SemaphoreType.DMA((2,)),
        ] + [pltpu.VMEM((SL, G, 128), jnp.float32)] * len(OUTER),
        compiler_params=SMALL,
    )(place, agg, first, second, *mid)


def unpack(packed):
    dims = (COLS * LA, NS // COLS, SL * NS)
    return pl.pallas_call(
        unpack_kernel,
        out_shape=shape(dims, jnp.float32),
        in_specs=[VMEM],
        out_specs=HBM,
        scratch_shapes=[pltpu.VMEM(dims, jnp.float32), pltpu.SemaphoreType.DMA((COLS,))],
        compiler_params=SMALL,
    )(packed)


def exchanged(shard, first):
    axis = ("rows", "cols")
    length = lax.axis_size(axis)
    pairs = [(i, (i + (1 if (i % 2 == 1) == first else -1)) % length) for i in range(length)]
    return lax.ppermute(shard, axis, pairs)


def shards(a_blocks, prolong, columns, aggregate):
    first, second, place, agg, p_v = load(prolong, aggregate, columns.T)
    first = exchanged(first, True)
    second = exchanged(second, False)
    mid = inner(place, agg, p_v, a_blocks)
    mine = outer(place, agg, first, second, *mid)
    landed = lax.all_to_all(mine, "cols", split_axis=0, concat_axis=0, tiled=True)
    return unpack(landed)


def solution(mesh):
    in_specs = (
        P(("rows", "cols"), None),
        P(("rows", "cols"), None),
        P(("rows", "cols"), None),
        P(("rows", "cols")),
    )
    out_specs = P("rows", "cols", None)
    return jax.shard_map(shards, mesh=mesh, in_specs=in_specs, out_specs=out_specs, check_vma=False)
```

```python
import jax
import jax.numpy as jnp
from jax import lax
from jax.experimental import pallas as pl
from jax.experimental.pallas import tpu as pltpu
from jax.sharding import PartitionSpec as P

BW = 64
NS = 64
KN = 7
HW = 8
RC = 2
SL = 5
LA = 4
NB = 32
G = BW // 2
BLK = BW * BW
COLS = 8
NONE = NB
LOW = NB + 1
HIGH = LOW + HW
PLACES = HIGH + HW
STEP = NB + 8
HALO_STEP = 2 * HW + 8
IDS = ((0, 2), (0, 3), (1, 3), (2, 2))
INNER = tuple(range(HW, NB - HW))
OUTER = tuple(range(HW)) + tuple(range(NB - HW, NB))

VMEM = pl.BlockSpec(memory_space=pltpu.VMEM)
HBM = pl.BlockSpec(memory_space=pltpu.HBM)
SMALL = pltpu.CompilerParams(vmem_limit_bytes=24 * 1024 * 1024)


def shape(dims, dtype):
    return jax.ShapeDtypeStruct(dims, dtype)


def low_lanes(rows):
    return lax.broadcasted_iota(jnp.int32, (rows, 128), 1) < NS


def above_first():
    return jnp.bitwise_and(lax.axis_index("cols"), 1) == 1


def load_kernel(p_hbm, agg_hbm, cols_hbm, first_ref, second_ref, place_ref, agg_ref, p_ref, agg_s, sems):
    p_in = pltpu.make_async_copy(p_hbm, p_ref, sems.at[0])
    ids_in = pltpu.make_async_copy(agg_hbm, agg_s, sems.at[1])
    cols_in = pltpu.make_async_copy(cols_hbm, place_ref, sems.at[2])
    agg_in = pltpu.make_async_copy(agg_hbm, agg_ref, sems.at[3])
    for c in (p_in, ids_in, cols_in, agg_in):
        c.start()
    ids_in.wait()
    last, first = jnp.int32(0), jnp.int32(0)
    for t in range(HW):
        last += (agg_s[NB - HW + t] == LA - 1).astype(jnp.int32)
        first += (agg_s[t] == 0).astype(jnp.int32)
    cols_in.wait()
    cols = place_ref[...]
    row = lax.broadcasted_iota(jnp.int32, cols.shape, 1)
    rel = row + jnp.bitwise_and(cols - row + HW, NB - 1) - HW
    place = jnp.where(rel < 0, rel + HW + LOW, jnp.where(rel < NB, rel, rel - NB + HIGH))
    place_ref[...] = jnp.where(cols < 0, NONE, place)
    p_in.wait()
    up_first = above_first()

    def fill(up_ref, down_ref):
        up_ref[:, :BLK] = p_ref[NB - HW:, :]
        up_ref[:, BLK:] = jnp.full((HW, 128), last.astype(jnp.float32), jnp.float32).astype(jnp.bfloat16)
        down_ref[:, :BLK] = p_ref[:HW, :]
        down_ref[:, BLK:] = jnp.full((HW, 128), first.astype(jnp.float32), jnp.float32).astype(jnp.bfloat16)

    pl.when(up_first)(lambda: fill(first_ref, second_ref))
    pl.when(jnp.logical_not(up_first))(lambda: fill(second_ref, first_ref))
    agg_in.wait()


def widen(nat, wide, low):
    even = jnp.where(low, nat, 0.0)
    odd = jnp.where(low, 0.0, nat)
    wide[pl.ds(0, G, stride=2), :] = even
    wide[pl.ds(1, G, stride=2), :] = pltpu.roll(odd, NS, 1)
    wide[pl.ds(BW, G, stride=2), :] = pltpu.roll(even, NS, 1)
    wide[pl.ds(BW + 1, G, stride=2), :] = odd


def products(rows, a_nat, w_ref, place_s, slot_of, accs):
    for k in range(KN):
        for i, acc in zip(rows, accs):
            block = a_nat[k, pl.ds(i, G, stride=STEP), :].astype(jnp.bfloat16)
            place = place_s[k, i]
            slot = slot_of(place, i)
            acc[slot] += jnp.dot(block, w_ref[place], preferred_element_type=jnp.float32)


def onto_coarse(groups, accs, sels):
    sums = {}
    low = low_lanes(NS)
    for at, group in enumerate(groups):
        first, count = IDS[group]
        mine = accs[at * 8:at * 8 + 8]
        parts = [
            lax.dot_general(jnp.concatenate([acc[s].astype(jnp.bfloat16) for acc in mine], axis=0), sels[at][...],
                            (((0,), (0,)), ((), ())), preferred_element_type=jnp.float32)
            for s in range(SL)
        ]
        full = jnp.concatenate(parts, axis=0)
        for c in range(count):
            cc = full[:, c * 128:(c + 1) * 128]
            part = lambda s, par: cc[s * 128 + par * NS:s * 128 + (par + 1) * NS]
            for pair in range(3):
                s0, s1 = 2 * pair, min(2 * pair + 1, SL - 1)
                stay = jnp.where(low, part(s0, 0), part(s1, 1))
                move = jnp.where(low, part(s1, 0), part(s0, 1))
                both = stay + pltpu.roll(move, NS, 1)
                key = (first + c, pair)
                sums[key] = sums[key] + both if key in sums else both
    return sums


def inner_kernel(place_v, agg_v, p_ref, a_hbm, a_nat, w_ref, sel_a, sel_d, part_ref, *scratch):
    a_ref, p_nat, wide, sel_b, sel_c, place_s, agg_s, glob, sems = scratch[:9]
    accs = scratch[9:]
    a_in = []
    for k in range(KN):
        part = (slice(None), pl.ds(k * BLK, BLK))
        a_in.append(pltpu.make_async_copy(a_hbm.at[part], a_ref.at[part], sems.at[2 + k]))
        a_in[k].start()
    place_in = pltpu.make_async_copy(place_v, place_s, sems.at[0])
    agg_in = pltpu.make_async_copy(agg_v, agg_s, sems.at[1])
    place_in.start()
    agg_in.start()
    for acc in accs:
        acc[...] = jnp.zeros_like(acc)
    sels = (sel_a, sel_b, sel_c, sel_d)
    for sel in sels:
        sel[...] = jnp.zeros_like(sel)
    for h in range(G):
        p_nat[pl.ds(h * STEP, NB), :] = p_ref[:, pl.ds(h * 128, 128)].astype(jnp.float32)
    place_in.wait()
    agg_in.wait()
    for t in range(NB):
        glob[t] = agg_s[t]
    glob[NONE] = 1
    low = low_lanes(G)
    for j in range(NB):
        nat = p_nat[pl.ds(j, G, stride=STEP), :]
        widen(nat, wide.at[j], low)
        w_ref[j] = wide[j].astype(jnp.bfloat16)
        lane = pl.multiple_of((agg_s[j] - IDS[j // 8][0]) * 128, 128)
        sels[j // 8][pl.ds(j % 8 * G, G), pl.ds(lane, 128)] = nat.astype(jnp.bfloat16)
    w_ref[NONE] = jnp.zeros((128, 128), jnp.bfloat16)
    for k in range(KN):
        a_in[k].wait()
        for g in range(G):
            a_nat[k, pl.ds(g * STEP, NB), :] = a_ref[:, pl.ds(k * BLK + g * 128, 128)].astype(jnp.float32)

    products(INNER, a_nat, w_ref, place_s, lambda place, i: glob[place] - agg_s[i] + RC, accs)
    for (c, pair), value in onto_coarse((1, 2), accs, (sel_b, sel_c)).items():
        part_ref[:, pl.ds(c * 8, 8), pl.ds(pair * 128, 128)] = value.reshape(8, 8, 128)


def outer_kernel(place_v, agg_v, first_ref, second_ref, a_nat, w_own, sel_a, sel_d, part_ref, out_ref, *scratch):
    p_nat, wide, w_all, place_s, agg_s, glob, sems = scratch[:7]
    accs = scratch[7:]
    place_in = pltpu.make_async_copy(place_v, place_s, sems.at[0])
    agg_in = pltpu.make_async_copy(agg_v, agg_s, sems.at[1])
    place_in.start()
    agg_in.start()
    up_first = above_first()
    in_first = jnp.max(first_ref[:, BLK:].astype(jnp.float32)).astype(jnp.int32)
    in_second = jnp.max(second_ref[:, BLK:].astype(jnp.float32)).astype(jnp.int32)
    below = jnp.where(up_first, in_second, in_first)
    above = jnp.where(up_first, in_first, in_second)
    at_first = pl.multiple_of(jnp.where(up_first, HW, 0), HW)
    at_second = pl.multiple_of(jnp.where(up_first, 0, HW), HW)
    for acc in accs:
        acc[...] = jnp.zeros_like(acc)
    for h in range(G):
        lanes = pl.ds(h * 128, 128)
        p_nat[pl.ds(h * HALO_STEP + at_first, HW), :] = first_ref[:, lanes].astype(jnp.float32)
        p_nat[pl.ds(h * HALO_STEP + at_second, HW), :] = second_ref[:, lanes].astype(jnp.float32)
    w_all[:LOW] = w_own[...]
    low = low_lanes(G)
    for j in range(2 * HW):
        widen(p_nat[pl.ds(j, G, stride=HALO_STEP), :], wide.at[j], low)
        w_all[LOW + j] = wide[j].astype(jnp.bfloat16)
    place_in.wait()
    agg_in.wait()
    for t in range(NB):
        glob[t] = agg_s[t]
    glob[NONE] = 1
    for t in range(HW):
        glob[LOW + t] = jnp.where(HW - t <= below, -1, -2)
        glob[HIGH + t] = jnp.where(t < above, LA, LA + 1)
    products(OUTER, a_nat, w_all, place_s, lambda place, i: glob[place] - agg_s[i] + RC, accs)
    sums = onto_coarse((0, 3), accs, (sel_a, sel_d))
    whole = {
        (c, pair): value.reshape(8, 8, 128) + part_ref[:, pl.ds(c * 8, 8), pl.ds(pair * 128, 128)]
        for (c, pair), value in sums.items()
    }
    for c in range(LA):
        both = jnp.concatenate([whole[c, 0], whole[c, 1]], axis=1)
        out_ref[:, pl.ds(c * 16, 16), :] = both.astype(jnp.bfloat16)
    low = low_lanes(8)[None]
    tails = [jnp.where(low, whole[c, 2], whole[c + 1, 2]) for c in range(0, LA, 2)]
    out_ref[:, pl.ds(LA * 16, 16), :] = jnp.concatenate(tails, axis=1).astype(jnp.bfloat16)


def unpack_kernel(packed_ref, out_hbm, rows_ref, sems):
    copies = []
    for z in range(COLS):
        packed = packed_ref[z].astype(jnp.float32)
        for c in range(LA):
            at = z * LA + c
            rows_ref[at, :, :128] = packed[c * 16:c * 16 + 8]
            rows_ref[at, :, 128:256] = packed[c * 16 + 8:c * 16 + 16]
            tail = packed[LA * 16 + c // 2 * 8:LA * 16 + c // 2 * 8 + 8]
            rows_ref[at, :, 256:] = (tail if c % 2 == 0 else pltpu.roll(tail, NS, 1))[:, :NS]
        part = pl.ds(z * LA, LA)
        copies.append(pltpu.make_async_copy(rows_ref.at[part], out_hbm.at[part], sems.at[z]))
        copies[z].start()
    for c in copies:
        c.wait()


def load(prolong, aggregate, columns_t):
    halo = shape((HW, BLK + 128), jnp.bfloat16)
    return pl.pallas_call(
        load_kernel,
        out_shape=(halo, halo, shape((KN, NB), jnp.int32), shape((NB,), jnp.int32), shape((NB, BLK), jnp.bfloat16)),
        in_specs=[HBM] * 3,
        out_specs=[VMEM] * 5,
        scratch_shapes=[pltpu.SMEM((NB,), jnp.int32), pltpu.SemaphoreType.DMA((4,))],
        compiler_params=SMALL,
    )(*(pltpu.with_memory_space_constraint(x, pltpu.HBM) for x in (prolong, aggregate, columns_t)))


def sel_shape(group):
    return 8 * G, IDS[group][1] * 128


def inner(place, agg, p_v, a_blocks):
    return pl.pallas_call(
        inner_kernel,
        out_shape=(shape((KN, G * STEP, 128), jnp.float32), shape((LOW, 128, 128), jnp.bfloat16),
                   shape(sel_shape(0), jnp.bfloat16), shape(sel_shape(3), jnp.bfloat16),
                   shape((COLS, LA * NS // COLS, 3 * 128), jnp.float32)),
        in_specs=[VMEM] * 3 + [HBM],
        out_specs=[VMEM] * 5,
        scratch_shapes=[
            pltpu.VMEM((NB, KN * BLK), jnp.bfloat16),
            pltpu.VMEM((G * STEP, 128), jnp.float32),
            pltpu.VMEM((NB, 128, 128), jnp.float32),
            pltpu.VMEM(sel_shape(1), jnp.bfloat16),
            pltpu.VMEM(sel_shape(2), jnp.bfloat16),
            pltpu.SMEM((KN, NB), jnp.int32),
            pltpu.SMEM((NB,), jnp.int32),
            pltpu.SMEM((PLACES,), jnp.int32),
            pltpu.SemaphoreType.DMA((2 + KN,)),
        ] + [pltpu.VMEM((SL, G, 128), jnp.float32)] * len(INNER),
        compiler_params=SMALL,
    )(place, agg, p_v, pltpu.with_memory_space_constraint(a_blocks, pltpu.HBM))


def outer(place, agg, first, second, *mid):
    return pl.pallas_call(
        outer_kernel,
        out_shape=shape((COLS, LA * 16 + 16, 128), jnp.bfloat16),
        in_specs=[VMEM] * 9,
        out_specs=VMEM,
        scratch_shapes=[
            pltpu.VMEM((G * HALO_STEP, 128), jnp.float32),
            pltpu.VMEM((2 * HW, 128, 128), jnp.float32),
            pltpu.VMEM((PLACES, 128, 128), jnp.bfloat16),
            pltpu.SMEM((KN, NB), jnp.int32),
            pltpu.SMEM((NB,), jnp.int32),
            pltpu.SMEM((PLACES,), jnp.int32),
            pltpu.SemaphoreType.DMA((2,)),
        ] + [pltpu.VMEM((SL, G, 128), jnp.float32)] * len(OUTER),
        compiler_params=SMALL,
    )(place, agg, first, second, *mid)


def unpack(packed):
    dims = (COLS * LA, NS // COLS, SL * NS)
    return pl.pallas_call(
        unpack_kernel,
        out_shape=shape(dims, jnp.float32),
        in_specs=[VMEM],
        out_specs=HBM,
        scratch_shapes=[pltpu.VMEM(dims, jnp.float32), pltpu.SemaphoreType.DMA((COLS,))],
        compiler_params=SMALL,
    )(packed)


def exchanged(shard, first):
    axis = ("rows", "cols")
    length = lax.axis_size(axis)
    pairs = [(i, (i + (1 if (i % 2 == 1) == first else -1)) % length) for i in range(length)]
    return lax.ppermute(shard, axis, pairs)


def shards(a_blocks, prolong, columns, aggregate):
    first, second, place, agg, p_v = load(prolong, aggregate, columns.T)
    first = exchanged(first, True)
    second = exchanged(second, False)
    mid = inner(place, agg, p_v, a_blocks)
    mine = outer(place, agg, first, second, *mid)
    landed = lax.all_to_all(mine, "cols", split_axis=0, concat_axis=0, tiled=True)
    return unpack(landed)


def solution(mesh):
    in_specs = (
        P(("rows", "cols"), None),
        P(("rows", "cols"), None),
        P(("rows", "cols"), None),
        P(("rows", "cols")),
    )
    out_specs = P("rows", "cols", None)
    return jax.shard_map(shards, mesh=mesh, in_specs=in_specs, out_specs=out_specs, check_vma=False)
```

```python
import jax
import jax.numpy as jnp
from jax import lax
from jax.experimental import pallas as pl
from jax.experimental.pallas import tpu as pltpu
from jax.sharding import PartitionSpec as P

BW = 64
NS = 64
KN = 7
HW = 8
RC = 2
SL = 5
LA = 4
NB = 32
G = BW // 2
BLK = BW * BW
COLS = 8
NONE = NB
LOW = NB + 1
HIGH = LOW + HW
PLACES = HIGH + HW
STEP = NB + 8
HALO_STEP = 2 * HW + 8
IDS = ((0, 2), (0, 3), (1, 3), (2, 2))
INNER = tuple(range(HW, NB - HW))
OUTER = tuple(range(HW)) + tuple(range(NB - HW, NB))

VMEM = pl.BlockSpec(memory_space=pltpu.VMEM)
HBM = pl.BlockSpec(memory_space=pltpu.HBM)
SMALL = pltpu.CompilerParams(vmem_limit_bytes=24 * 1024 * 1024)


def shape(dims, dtype):
    return jax.ShapeDtypeStruct(dims, dtype)


def low_lanes(rows):
    return lax.broadcasted_iota(jnp.int32, (rows, 128), 1) < NS


def above_first():
    return jnp.bitwise_and(lax.axis_index("cols"), 1) == 1


def load_kernel(p_hbm, agg_hbm, cols_hbm, first_ref, second_ref, place_ref, agg_ref, p_ref, agg_s, sems):
    p_in = pltpu.make_async_copy(p_hbm, p_ref, sems.at[0])
    ids_in = pltpu.make_async_copy(agg_hbm, agg_s, sems.at[1])
    cols_in = pltpu.make_async_copy(cols_hbm, place_ref, sems.at[2])
    agg_in = pltpu.make_async_copy(agg_hbm, agg_ref, sems.at[3])
    for c in (p_in, ids_in, cols_in, agg_in):
        c.start()
    ids_in.wait()
    last, first = jnp.int32(0), jnp.int32(0)
    for t in range(HW):
        last += (agg_s[NB - HW + t] == LA - 1).astype(jnp.int32)
        first += (agg_s[t] == 0).astype(jnp.int32)
    cols_in.wait()
    cols = place_ref[...]
    row = lax.broadcasted_iota(jnp.int32, cols.shape, 1)
    rel = row + jnp.bitwise_and(cols - row + HW, NB - 1) - HW
    place = jnp.where(rel < 0, rel + HW + LOW, jnp.where(rel < NB, rel, rel - NB + HIGH))
    place_ref[...] = jnp.where(cols < 0, NONE, place)
    p_in.wait()
    up_first = above_first()

    def fill(up_ref, down_ref):
        up_ref[:, :BLK] = p_ref[NB - HW:, :]
        up_ref[:, BLK:] = jnp.full((HW, 128), last.astype(jnp.float32), jnp.float32).astype(jnp.bfloat16)
        down_ref[:, :BLK] = p_ref[:HW, :]
        down_ref[:, BLK:] = jnp.full((HW, 128), first.astype(jnp.float32), jnp.float32).astype(jnp.bfloat16)

    pl.when(up_first)(lambda: fill(first_ref, second_ref))
    pl.when(jnp.logical_not(up_first))(lambda: fill(second_ref, first_ref))
    agg_in.wait()


def widen(nat, wide, low):
    even = jnp.where(low, nat, 0.0)
    odd = jnp.where(low, 0.0, nat)
    wide[pl.ds(0, G, stride=2), :] = even
    wide[pl.ds(1, G, stride=2), :] = pltpu.roll(odd, NS, 1)
    wide[pl.ds(BW, G, stride=2), :] = pltpu.roll(even, NS, 1)
    wide[pl.ds(BW + 1, G, stride=2), :] = odd


def products(rows, a_nat, w_ref, place_s, slot_of, accs, entries=range(KN)):
    for k in entries:
        for i, acc in zip(rows, accs):
            block = a_nat[k, pl.ds(i, G, stride=STEP), :].astype(jnp.bfloat16)
            place = place_s[k, i]
            slot = slot_of(place, i)
            acc[slot] += jnp.dot(block, w_ref[place], preferred_element_type=jnp.float32)


def onto_coarse(groups, accs, sels):
    sums = {}
    low = low_lanes(NS)
    for at, group in enumerate(groups):
        first, count = IDS[group]
        mine = accs[at * 8:at * 8 + 8]
        rows = [jnp.concatenate([acc[s] for s in range(SL)], axis=1).astype(jnp.bfloat16) for acc in mine]
        full = lax.dot_general(jnp.concatenate(rows, axis=0), sels[at][...], (((0,), (0,)), ((), ())),
                               preferred_element_type=jnp.float32)
        for c in range(count):
            cc = full[:, c * 128:(c + 1) * 128]
            part = lambda s, par: cc[s * 128 + par * NS:s * 128 + (par + 1) * NS]
            for pair in range(3):
                s0, s1 = 2 * pair, min(2 * pair + 1, SL - 1)
                stay = jnp.where(low, part(s0, 0), part(s1, 1))
                move = jnp.where(low, part(s1, 0), part(s0, 1))
                both = stay + pltpu.roll(move, NS, 1)
                key = (first + c, pair)
                sums[key] = sums[key] + both if key in sums else both
    return sums


def inner_kernel(place_v, agg_v, p_ref, a_hbm, a_nat, w_ref, sel_a, sel_d, part_ref, *scratch):
    a_ref, p_nat, wide, sel_b, sel_c, place_s, agg_s, glob, sems = scratch[:9]
    accs = scratch[9:]
    a_in = []
    for k in range(KN):
        part = (slice(None), pl.ds(k * BLK, BLK))
        a_in.append(pltpu.make_async_copy(a_hbm.at[part], a_ref.at[part], sems.at[2 + k]))
        a_in[k].start()
    place_in = pltpu.make_async_copy(place_v, place_s, sems.at[0])
    agg_in = pltpu.make_async_copy(agg_v, agg_s, sems.at[1])
    place_in.start()
    agg_in.start()
    for acc in accs:
        acc[...] = jnp.zeros_like(acc)
    sels = (sel_a, sel_b, sel_c, sel_d)
    for sel in sels:
        sel[...] = jnp.zeros_like(sel)
    for h in range(G):
        p_nat[pl.ds(h * STEP, NB), :] = p_ref[:, pl.ds(h * 128, 128)].astype(jnp.float32)
    place_in.wait()
    agg_in.wait()
    for t in range(NB):
        glob[t] = agg_s[t]
    glob[NONE] = 1
    low = low_lanes(G)
    for j in range(NB):
        nat = p_nat[pl.ds(j, G, stride=STEP), :]
        widen(nat, wide.at[j], low)
        w_ref[j] = wide[j].astype(jnp.bfloat16)
        lane = pl.multiple_of((agg_s[j] - IDS[j // 8][0]) * 128, 128)
        sels[j // 8][pl.ds(j % 8 * G, G), pl.ds(lane, 128)] = nat.astype(jnp.bfloat16)
    w_ref[NONE] = jnp.zeros((128, 128), jnp.bfloat16)

    for entries in (range(3), range(3, KN)):
        for k in entries:
            a_in[k].wait()
            for g in range(G):
                a_nat[k, pl.ds(g * STEP, NB), :] = a_ref[:, pl.ds(k * BLK + g * 128, 128)].astype(jnp.float32)
        products(INNER, a_nat, w_ref, place_s, lambda place, i: glob[place] - agg_s[i] + RC, accs, entries)
    for (c, pair), value in onto_coarse((1, 2), accs, (sel_b, sel_c)).items():
        part_ref[:, pl.ds(c * 8, 8), pl.ds(pair * 128, 128)] = value.reshape(8, 8, 128)


def outer_kernel(place_v, agg_v, first_ref, second_ref, a_nat, w_own, sel_a, sel_d, part_ref, out_ref, *scratch):
    p_nat, wide, w_all, place_s, agg_s, glob, sems = scratch[:7]
    accs = scratch[7:]
    place_in = pltpu.make_async_copy(place_v, place_s, sems.at[0])
    agg_in = pltpu.make_async_copy(agg_v, agg_s, sems.at[1])
    place_in.start()
    agg_in.start()
    up_first = above_first()
    in_first = jnp.max(first_ref[:, BLK:].astype(jnp.float32)).astype(jnp.int32)
    in_second = jnp.max(second_ref[:, BLK:].astype(jnp.float32)).astype(jnp.int32)
    below = jnp.where(up_first, in_second, in_first)
    above = jnp.where(up_first, in_first, in_second)
    at_first = pl.multiple_of(jnp.where(up_first, HW, 0), HW)
    at_second = pl.multiple_of(jnp.where(up_first, 0, HW), HW)
    for acc in accs:
        acc[...] = jnp.zeros_like(acc)
    for h in range(G):
        lanes = pl.ds(h * 128, 128)
        p_nat[pl.ds(h * HALO_STEP + at_first, HW), :] = first_ref[:, lanes].astype(jnp.float32)
        p_nat[pl.ds(h * HALO_STEP + at_second, HW), :] = second_ref[:, lanes].astype(jnp.float32)
    w_all[:LOW] = w_own[...]
    low = low_lanes(G)
    for j in range(2 * HW):
        widen(p_nat[pl.ds(j, G, stride=HALO_STEP), :], wide.at[j], low)
        w_all[LOW + j] = wide[j].astype(jnp.bfloat16)
    place_in.wait()
    agg_in.wait()
    for t in range(NB):
        glob[t] = agg_s[t]
    glob[NONE] = 1
    for t in range(HW):
        glob[LOW + t] = jnp.where(HW - t <= below, -1, -2)
        glob[HIGH + t] = jnp.where(t < above, LA, LA + 1)
    products(OUTER, a_nat, w_all, place_s, lambda place, i: glob[place] - agg_s[i] + RC, accs)
    sums = onto_coarse((0, 3), accs, (sel_a, sel_d))
    whole = {
        (c, pair): value.reshape(8, 8, 128) + part_ref[:, pl.ds(c * 8, 8), pl.ds(pair * 128, 128)]
        for (c, pair), value in sums.items()
    }
    for c in range(LA):
        both = jnp.concatenate([whole[c, 0], whole[c, 1]], axis=1)
        out_ref[:, pl.ds(c * 16, 16), :] = both.astype(jnp.bfloat16)
    low = low_lanes(8)[None]
    tails = [jnp.where(low, whole[c, 2], whole[c + 1, 2]) for c in range(0, LA, 2)]
    out_ref[:, pl.ds(LA * 16, 16), :] = jnp.concatenate(tails, axis=1).astype(jnp.bfloat16)


def unpack_kernel(packed_ref, out_hbm, rows_ref, sems):
    copies = []
    for z in range(COLS):
        packed = packed_ref[z].astype(jnp.float32)
        for c in range(LA):
            at = z * LA + c
            rows_ref[at, :, :128] = packed[c * 16:c * 16 + 8]
            rows_ref[at, :, 128:256] = packed[c * 16 + 8:c * 16 + 16]
            tail = packed[LA * 16 + c // 2 * 8:LA * 16 + c // 2 * 8 + 8]
            rows_ref[at, :, 256:] = (tail if c % 2 == 0 else pltpu.roll(tail, NS, 1))[:, :NS]
        part = pl.ds(z * LA, LA)
        copies.append(pltpu.make_async_copy(rows_ref.at[part], out_hbm.at[part], sems.at[z]))
        copies[z].start()
    for c in copies:
        c.wait()


def load(prolong, aggregate, columns_t):
    halo = shape((HW, BLK + 128), jnp.bfloat16)
    return pl.pallas_call(
        load_kernel,
        out_shape=(halo, halo, shape((KN, NB), jnp.int32), shape((NB,), jnp.int32), shape((NB, BLK), jnp.bfloat16)),
        in_specs=[HBM] * 3,
        out_specs=[VMEM] * 5,
        scratch_shapes=[pltpu.SMEM((NB,), jnp.int32), pltpu.SemaphoreType.DMA((4,))],
        compiler_params=SMALL,
    )(*(pltpu.with_memory_space_constraint(x, pltpu.HBM) for x in (prolong, aggregate, columns_t)))


def sel_shape(group):
    return 8 * G, IDS[group][1] * 128


def inner(place, agg, p_v, a_blocks):
    return pl.pallas_call(
        inner_kernel,
        out_shape=(shape((KN, G * STEP, 128), jnp.float32), shape((LOW, 128, 128), jnp.bfloat16),
                   shape(sel_shape(0), jnp.bfloat16), shape(sel_shape(3), jnp.bfloat16),
                   shape((COLS, LA * NS // COLS, 3 * 128), jnp.float32)),
        in_specs=[VMEM] * 3 + [HBM],
        out_specs=[VMEM] * 5,
        scratch_shapes=[
            pltpu.VMEM((NB, KN * BLK), jnp.bfloat16),
            pltpu.VMEM((G * STEP, 128), jnp.float32),
            pltpu.VMEM((NB, 128, 128), jnp.float32),
            pltpu.VMEM(sel_shape(1), jnp.bfloat16),
            pltpu.VMEM(sel_shape(2), jnp.bfloat16),
            pltpu.SMEM((KN, NB), jnp.int32),
            pltpu.SMEM((NB,), jnp.int32),
            pltpu.SMEM((PLACES,), jnp.int32),
            pltpu.SemaphoreType.DMA((2 + KN,)),
        ] + [pltpu.VMEM((SL, G, 128), jnp.float32)] * len(INNER),
        compiler_params=SMALL,
    )(place, agg, p_v, pltpu.with_memory_space_constraint(a_blocks, pltpu.HBM))


def outer(place, agg, first, second, *mid):
    return pl.pallas_call(
        outer_kernel,
        out_shape=shape((COLS, LA * 16 + 16, 128), jnp.bfloat16),
        in_specs=[VMEM] * 9,
        out_specs=VMEM,
        scratch_shapes=[
            pltpu.VMEM((G * HALO_STEP, 128), jnp.float32),
            pltpu.VMEM((2 * HW, 128, 128), jnp.float32),
            pltpu.VMEM((PLACES, 128, 128), jnp.bfloat16),
            pltpu.SMEM((KN, NB), jnp.int32),
            pltpu.SMEM((NB,), jnp.int32),
            pltpu.SMEM((PLACES,), jnp.int32),
            pltpu.SemaphoreType.DMA((2,)),
        ] + [pltpu.VMEM((SL, G, 128), jnp.float32)] * len(OUTER),
        compiler_params=SMALL,
    )(place, agg, first, second, *mid)


def unpack(packed):
    dims = (COLS * LA, NS // COLS, SL * NS)
    return pl.pallas_call(
        unpack_kernel,
        out_shape=shape(dims, jnp.float32),
        in_specs=[VMEM],
        out_specs=HBM,
        scratch_shapes=[pltpu.VMEM(dims, jnp.float32), pltpu.SemaphoreType.DMA((COLS,))],
        compiler_params=SMALL,
    )(packed)


def exchanged(shard, first):
    axis = ("rows", "cols")
    length = lax.axis_size(axis)
    pairs = [(i, (i + (1 if (i % 2 == 1) == first else -1)) % length) for i in range(length)]
    return lax.ppermute(shard, axis, pairs)


def shards(a_blocks, prolong, columns, aggregate):
    first, second, place, agg, p_v = load(prolong, aggregate, columns.T)
    first = exchanged(first, True)
    second = exchanged(second, False)
    mid = inner(place, agg, p_v, a_blocks)
    mine = outer(place, agg, first, second, *mid)
    landed = lax.all_to_all(mine, "cols", split_axis=0, concat_axis=0, tiled=True)
    return unpack(landed)


def solution(mesh):
    in_specs = (
        P(("rows", "cols"), None),
        P(("rows", "cols"), None),
        P(("rows", "cols"), None),
        P(("rows", "cols")),
    )
    out_specs = P("rows", "cols", None)
    return jax.shard_map(shards, mesh=mesh, in_specs=in_specs, out_specs=out_specs, check_vma=False)
```
